256 devices in a mesh: size: 4 (over x_hi, core), gz: 64 (over z, y, x_lo).
Axes of the slice: x: 4 (x_hi: 2, x_lo: 2; x = x_hi * 2 + x_lo), y: 4, z: 8, core: 2. Of those that a mesh axis runs over, the one named last changes fastest.
Arguments:
- concentration: float32 [8, 256, 128, 128], P('size', 'gz'), may hold values from 0 to 2
- deposit: float32 [8, 256, 128, 128], P('size', 'gz'), may hold values from 0 to 1
- velocity: float32 [256, 128, 128], P('gz'), may hold values from 0.2 to 1
- pore_label: int32 [256, 128, 128], P('gz'), may hold values from 0 to 3
- diffusivity: float32 [8], P('size'), may hold values from 0.15 to 0.5
- attach_rate: float32 [8], P('size'), may hold values from 0.4 to 4
- volume: float32 [8], P('size'), may hold values from 0.05 to 0.3
- conc_cotangent: float32 [8, 256, 128, 128], P('size', 'gz'), may hold values from -6 to 6
- deposit_cotangent: float32 [8, 256, 128, 128], P('size', 'gz'), may hold values from -6 to 6
Outputs:
- conc_adjoint: float32 [8, 256, 128, 128], P('size', 'gz')
- deposit_adjoint: float32 [8, 256, 128, 128], P('size', 'gz')
The draws below stay inside these ranges and needn't reach their ends.
All inputs are finite; a program needn't handle non-finite values.
Results may differ from the reference program's by a relative error of at most 0.0001.
Values sent between devices are 32-bit elements; how exact they have to be, the bound alone decides.
No kernel may reach another device: no remote copies, remote signals or barrier semaphores. Data moves between devices by JAX's collectives and lax.ppermute only.
A program may use at most 64 MiB of HBM per device.

```python
import math
import jax
import jax.numpy as jnp

CLASSES = 8
NX = 128
NY = 128
NZ = 256


def plant(array, stream_key, low, largest):
    spot = [jax.random.randint(jax.random.fold_in(stream_key, axis), (), 0, length) for axis, length in enumerate(array.shape)]
    longest = array.shape.index(max(array.shape))
    neighbour = spot[:longest] + [(spot[longest] + 1) % array.shape[longest]] + spot[longest + 1:]
    return array.at[tuple(spot)].set(low).at[tuple(neighbour)].set(largest)


def level_of(stream_key, shape, split, smallest, high):
    gain = 1.0
    for position, blocks in split:
        steps = jax.random.uniform(jax.random.fold_in(jax.random.fold_in(stream_key, 6), position), (blocks,), jnp.float32, smallest / len(split), high / len(split))
        gain = gain * jnp.repeat(jnp.exp(steps), shape[position] // blocks).reshape((-1,) + (1,) * (len(shape) - 1 - position))
    return gain


def gaussian(key, shape, scale, reach, shards=(), kind=jnp.bfloat16):
    factor_of = level_of(key, shape, shards, -0.22, 0.18) if shards else 1.0
    drawn = jax.random.normal(key, shape, jnp.float32) * scale * factor_of
    return jnp.minimum(jnp.maximum(drawn, -reach), reach).astype(kind)


def setup_inputs(seed: int = 0) -> dict:
    key_of = jax.random.split(jax.random.key(seed), 10)
    return {
        "concentration": jnp.clip(2.0 * jax.random.uniform(key_of[0], (CLASSES, NZ, NX, NY), jnp.float32) ** level_of(key_of[0], (CLASSES, NZ, NX, NY), ((0, 4), (1, 64)), -0.2, 0.2), 0.0, 2.0),
        "deposit": jnp.clip(1.0 * jax.random.uniform(key_of[1], (CLASSES, NZ, NX, NY), jnp.float32) ** level_of(key_of[1], (CLASSES, NZ, NX, NY), ((0, 4), (1, 64)), -0.2, 0.2), 0.0, 1.0),
        "velocity": jnp.clip(0.2 + 0.8 * jax.random.uniform(key_of[2], (NZ, NX, NY), jnp.float32) ** level_of(key_of[2], (NZ, NX, NY), ((0, 64),), -0.2, 0.2), 0.2, 1.0),
        "pore_label": plant(jax.random.randint(key_of[3], (NZ, NX, NY), 0, 4), jax.random.fold_in(key_of[3], 1), 0, 3).astype(jnp.int32),
        "diffusivity": jnp.clip(jnp.exp(math.log(0.5) - 1.2039728 * jax.random.uniform(key_of[4], (CLASSES,), jnp.float32) ** level_of(key_of[4], (CLASSES,), ((0, 4),), -0.2, 0.2)), 0.15, 0.5),
        "attach_rate": jnp.clip(jnp.exp(math.log(4.0) - 2.3025851 * jax.random.uniform(key_of[5], (CLASSES,), jnp.float32) ** level_of(key_of[5], (CLASSES,), ((0, 4),), -0.2, 0.2)), 0.4, 4.0),
        "volume": jnp.clip(jnp.exp(math.log(0.3) - 1.7917595 * jax.random.uniform(key_of[6], (CLASSES,), jnp.float32) ** level_of(key_of[6], (CLASSES,), ((0, 4),), -0.2, 0.2)), 0.05, 0.3),
        "conc_cotangent": gaussian(key_of[7], (CLASSES, NZ, NX, NY), 1.0, 6.0, ((0, 4), (1, 64)), jnp.float32),
        "deposit_cotangent": gaussian(key_of[8], (CLASSES, NZ, NX, NY), 1.0, 6.0, ((0, 4), (1, 64)), jnp.float32),
    }


CLOGGING = 1.0
TIME_STEP = 0.25
SURFACE_EFF = (0.1, 0.6, 1.2, 2.0)
MIXING = ((0.0, 1.0), (0.75, 0.25), (1.0 / 3.0, 2.0 / 3.0))


def efficiency(labels):
    result = jnp.zeros(labels.shape, jnp.float32)
    for label_value in range(4):
        result = result + SURFACE_EFF[label_value] * (labels == label_value).astype(jnp.float32)
    return result


def laplacian(field):
    padded = jnp.pad(field, ((0, 0), (1, 1), (1, 1), (1, 1)))
    middle = padded[:, 1:-1, 1:-1, 1:-1]
    return (padded[:, 2:, 1:-1, 1:-1] + padded[:, :-2, 1:-1, 1:-1]
            + padded[:, 1:-1, 2:, 1:-1] + padded[:, 1:-1, :-2, 1:-1]
            + padded[:, 1:-1, 1:-1, 2:] + padded[:, 1:-1, 1:-1, :-2] - 6.0 * middle)


def below(field):
    return jnp.pad(field, ((0, 0), (1, 0), (0, 0), (0, 0)))[:, :-1]


def above(field):
    return jnp.pad(field, ((0, 0), (0, 1), (0, 0), (0, 0)))[:, 1:]


def reference(concentration, deposit, velocity, pore_label, diffusivity, attach_rate, volume, conc_cotangent, deposit_cotangent):
    collector = efficiency(pore_label)[None]
    coeff_dif = diffusivity[:, None, None, None]
    coeff_rate = attach_rate[:, None, None, None]
    coeff_vol = volume[:, None, None, None]
    flow_here = velocity[None]

    def blocking(dep_state):
        return jnp.exp(-CLOGGING * jnp.sum(coeff_vol * dep_state, axis=0))[None]

    conc_states = [concentration]
    dep_states = [deposit]
    blocks = []
    for segment_index in range(3):
        blocked = blocking(dep_states[-1])
        blocks.append(blocked)
        if segment_index < 2:
            conc_now = conc_states[-1]
            reaction = coeff_rate * collector * blocked * conc_now
            rate_conc = coeff_dif * laplacian(conc_now) - flow_here * (conc_now - below(conc_now)) - reaction
            weight_old, weight_new = MIXING[segment_index]
            conc_states.append(weight_old * concentration + weight_new * (conc_now + TIME_STEP * rate_conc))
            dep_states.append(weight_old * deposit + weight_new * (dep_states[-1] + TIME_STEP * reaction))

    def adjoint(push_conc, push_dep, conc_state, blocked):
        uptake = coeff_rate * collector * blocked
        weight = push_dep - push_conc
        back_conc = (coeff_dif * laplacian(push_conc) - flow_here * push_conc
                     + above(flow_here * push_conc) + uptake * weight)
        theta_grad = -CLOGGING * jnp.sum(weight * (uptake * conc_state), axis=0)
        return back_conc, coeff_vol * theta_grad[None]

    adj_conc = conc_cotangent
    adj_dep = deposit_cotangent
    total_conc = jnp.zeros(concentration.shape, jnp.float32)
    total_dep = jnp.zeros(deposit.shape, jnp.float32)
    for segment_index in (2, 1, 0):
        weight_old, weight_new = MIXING[segment_index]
        back_conc, back_dep = adjoint(weight_new * TIME_STEP * adj_conc, weight_new * TIME_STEP * adj_dep,
                                      conc_states[segment_index], blocks[segment_index])
        total_conc = total_conc + weight_old * adj_conc
        total_dep = total_dep + weight_old * adj_dep
        adj_conc = weight_new * adj_conc + back_conc
        adj_dep = weight_new * adj_dep + back_dep
    return total_conc + adj_conc, total_dep + adj_dep
```

```python
import functools

import jax
import jax.numpy as jnp
from jax import lax
from jax.experimental import pallas as pl
from jax.experimental.pallas import tpu as pltpu
from jax.sharding import PartitionSpec as P

H = 0.25
SURFACE_EFF = (0.1, 0.6, 1.2, 2.0)
N = 128
F32 = jnp.float32


def lateral(x):
    row = lax.broadcasted_iota(jnp.int32, x.shape, 0)
    col = lax.broadcasted_iota(jnp.int32, x.shape, 1)
    up = jnp.where(row > 0, pltpu.roll(x, 1, 0), 0.0)
    down = jnp.where(row < N - 1, pltpu.roll(x, N - 1, 0), 0.0)
    left = jnp.where(col > 0, pltpu.roll(x, 1, 1), 0.0)
    right = jnp.where(col < N - 1, pltpu.roll(x, N - 1, 1), 0.0)
    return (up + down) + (left + right) - 6.0 * x


def efficiency(label):
    out = jnp.zeros(label.shape, F32)
    for k in range(4):
        out = jnp.where(label == k, SURFACE_EFF[k], out)
    return out


class Coef:
    def __init__(self, ref):
        self.dif = [ref[c : c + 1, :] for c in range(4)]
        self.rate = [ref[4 + c : 5 + c, :] for c in range(4)]
        self.vol = [ref[8 + c : 9 + c, :] for c in range(4)]


def send_state(core_ref, dif, rate, vol, dep, conc, msg):
    other = 1 - core_ref[0]
    for l in range(2):
        msg[l] = vol[0] * dep[0, 2 * other + l] + vol[1] * dep[1, 2 * other + l]
    for c in range(2):
        for l in range(2):
            msg[2 + 3 * c + l] = conc[c, 2 * other + l]
        msg[4 + 3 * c] = conc[c, 2 - other]
    for k, ref in enumerate((dif, rate, vol)):
        for c in range(2):
            msg[8, 2 * k + c : 2 * k + c + 1, :] = jnp.full((1, N), ref[c], F32)


def send_cot(core_ref, p, q, msg):
    other = 1 - core_ref[0]
    for c in range(2):
        for l in range(2):
            msg[3 * c + l] = p[c, 2 * other + l]
            msg[6 + 2 * c + l] = q[c, 2 * other + l]
        msg[3 * c + 2] = p[c, 2 - other]


def sums_zero(core_ref, dif, rate, vol, dep, conc, got, pk1, ho, c0, coef, u4, uin):
    core = core_ref[0]
    for k, ref in enumerate((dif, rate, vol)):
        for c in range(2):
            coef[4 * k + c : 4 * k + c + 1, :] = jnp.full((1, N), ref[c], F32)
            coef[4 * k + 2 + c : 4 * k + 3 + c, :] = got[8, 2 * k + c : 2 * k + c + 1, :]
    co = Coef(coef)
    for l in range(2):
        pk1[l] = got[l] + vol[0] * dep[0, 2 * core + l] + vol[1] * dep[1, 2 * core + l]
        total = jnp.zeros((N, N), F32)
        square = jnp.zeros((N, N), F32)
        for c in range(4):
            u = conc[c, 2 * core + l] if c < 2 else got[2 + 3 * (c - 2) + l]
            u4[c, l] = u
            term = (co.vol[c] * co.rate[c]) * u
            total = total + term
            square = square + co.rate[c] * term
        pk1[2 + l] = total
        c0[l] = square
    for c in range(4):
        uin[c] = conc[c, 2 - core] if c < 2 else got[4 + 3 * (c - 2)]
        ho[(c + 2) % 4] = u4[c, core]


def advect(co, u4, vel, core, c, l):
    u = u4[c, l]
    out = co.dif[c] * lateral(u) - vel[2 * core + l] * u
    if l == 0:
        return out + co.dif[c] * u4[c, 1]
    return out + (co.dif[c] + vel[2 * core + 1]) * u4[c, 0]


def back(co, x4, vel, core, c, l):
    x = x4[c, l]
    out = co.dif[c] * lateral(x) - vel[2 * core + l] * x
    if l == 0:
        return out + (co.dif[c] + vel[2 * core + 1]) * x4[c, 1]
    return out + co.dif[c] * x4[c, 0]


def facing(co, vel, core):
    low = vel[2 * core]
    out_part = jnp.where(core == 0, low, 0.0)
    in_part = jnp.where(core == 1, low, 0.0)
    return (
        [co.dif[c] + out_part for c in range(4)],
        [co.dif[c] + in_part for c in range(4)],
    )


def step_base(core_ref, coef, u4, uin, vel, a4):
    core = core_ref[0]
    co = Coef(coef)
    _, fin = facing(co, vel, core)
    for c in range(4):
        for l in range(2):
            a4[c, l] = u4[c, l] + H * advect(co, u4, vel, core, c, l)
        a4[c, 1 - core] = a4[c, 1 - core] + H * (fin[c] * uin[c])


def cot_base(core_ref, coef, p, q, got, vel, p4, q4, base, ho):
    core = core_ref[0]
    co = Coef(coef)
    fout, _ = facing(co, vel, core)
    inner = 2 - core
    above = jnp.where(core == 0, vel[inner], 0.0)
    for c in range(4):
        for l in range(2):
            p4[c, l] = p[c, 2 * core + l] if c < 2 else got[3 * (c - 2) + l]
            q4[c, l] = q[c, 2 * core + l] if c < 2 else got[6 + 2 * (c - 2) + l]
        for l in range(2):
            base[c, l] = back(co, p4, vel, core, c, l)
        pin = p[c, inner] if c < 2 else got[3 * (c - 2) + 2]
        base[c, 1 - core] = base[c, 1 - core] + (co.dif[c] + above) * pin
        ho[(c + 2) % 4] = fout[c] * p4[c, core]


def sums_one(core_ref, coef, base, hout, vel, c0, a4, pk2):
    core = core_ref[0]
    co = Coef(coef)
    fout, _ = facing(co, vel, core)
    for l in range(2):
        for c in range(4):
            a4[c, l] = base[c, l]
    for c in range(4):
        a4[c, core] = a4[c, core] + H * (fout[c] * hout[c])
    for l in range(2):
        total = jnp.zeros((N, N), F32)
        for c in range(4):
            total = total + (co.vol[c] * co.rate[c]) * a4[c, l]
        pk2[l] = total
        pk2[2 + l] = c0[l]


def state_one(core_ref, coef, pk1, got, label, a4, u4, u1, ho, hi, k01, th, asum):
    core = core_ref[0]
    co = Coef(coef)
    for l in range(2):
        coll = efficiency(label[2 * core + l])
        theta = pk1[l] + got[l]
        a0 = pk1[2 + l] + got[2 + l]
        k0 = coll * jnp.exp(-theta)
        theta1 = theta + H * (k0 * a0)
        k01[l] = k0
        k01[2 + l] = coll * jnp.exp(-theta1)
        k01[4 + l] = coll
        th[l] = theta
        th[2 + l] = theta1
        asum[l] = a0
        for c in range(4):
            u1[c, l] = a4[c, l] - (H * k0) * (co.rate[c] * u4[c, l])
    for c in range(4):
        ho[(c + 2) % 4] = u1[c, core]
        hi[(c + 2) % 4] = u1[c, 1 - core]


def cot_two(core_ref, coef, pk2, got, k01, th, p4, q4, base, hout, vel, u1, l2, ho, hi, s1, kk, asum):
    core = core_ref[0]
    co = Coef(coef)
    fout, fin = facing(co, vel, core)
    for l in range(2):
        g0 = pk2[l] + got[l]
        c0 = pk2[2 + l] + got[2 + l]
        a1 = g0 - (H * k01[l]) * c0
        theta2 = 0.75 * th[l] + 0.25 * (th[2 + l] + H * (k01[2 + l] * a1))
        k2 = k01[4 + l] * jnp.exp(-theta2)
        asum[l] = a1
        asum[2 + l] = c0
        kk[l] = k2
        for c in range(4):
            p = p4[c, l]
            l2[c, l] = (2.0 / 3.0) * p + (2.0 / 3.0 * H) * (
                base[c, l] + (co.rate[c] * k2) * (q4[c, l] - p)
            )
    for c in range(4):
        l2[c, core] = l2[c, core] + (2.0 / 3.0 * H) * hout[c]
        ho[(c + 2) % 4] = fout[c] * l2[c, core]
        hi[(c + 2) % 4] = fin[c] * l2[c, 1 - core]
    for l in range(2):
        total = jnp.zeros((N, N), F32)
        for c in range(4):
            total = total + ((2.0 / 3.0) * q4[c, l] - l2[c, l]) * (co.rate[c] * u1[c, l])
        s1[l] = total


def sums_two(core_ref, coef, u4, u1, hout, hin, k01, vel, p4, q4, s1, pk3, tmp):
    core = core_ref[0]
    co = Coef(coef)
    fout, fin = facing(co, vel, core)
    for c in range(4):
        for l in range(2):
            tmp[c, l] = advect(co, u1, vel, core, c, l)
        tmp[c, core] = tmp[c, core] + fout[c] * hout[c]
        tmp[c, 1 - core] = tmp[c, 1 - core] + fin[c] * hin[c]
    for l in range(2):
        total = jnp.zeros((N, N), F32)
        for c in range(4):
            u = u1[c, l]
            rate = tmp[c, l] - (co.rate[c] * k01[2 + l]) * u
            u2 = 0.75 * u4[c, l] + 0.25 * (u + H * rate)
            total = total + (q4[c, l] - p4[c, l]) * (co.rate[c] * u2)
        pk3[l] = total
        pk3[2 + l] = s1[l]


def sums_three(core_ref, coef, l2, hout, hin, k01, vel, q4, u4, l1, s0):
    core = core_ref[0]
    co = Coef(coef)
    for c in range(4):
        for l in range(2):
            l1[c, l] = back(co, l2, vel, core, c, l)
        l1[c, core] = l1[c, core] + hout[c]
        l1[c, 1 - core] = l1[c, 1 - core] + hin[c]
    for l in range(2):
        total = jnp.zeros((N, N), F32)
        for c in range(4):
            x = l2[c, l]
            w = (2.0 / 3.0) * q4[c, l] - x
            y = 0.25 * x + (0.25 * H) * (l1[c, l] + (co.rate[c] * k01[2 + l]) * w)
            l1[c, l] = y
            total = total + (q4[c, l] * (1.0 / 6.0) - y) * (co.rate[c] * u4[c, l])
        s0[l] = total


def cot_one(core_ref, coef, pk3, got, k01, kk, asum, l1k, vel, l1, ho, hi, tt):
    core = core_ref[0]
    co = Coef(coef)
    fout, fin = facing(co, vel, core)
    for l in range(2):
        t2 = (-2.0 / 3.0 * H) * kk[l] * (pk3[l] + got[l])
        s1 = pk3[2 + l] + got[2 + l]
        t1 = (-0.25 * H) * k01[2 + l] * (s1 + t2 * asum[l])
        tt[l] = t2
        tt[2 + l] = t1
        push = (0.25 * H) * (k01[2 + l] * t2)
        for c in range(4):
            l1[c, l] = l1k[c, l] + (co.rate[c] * co.vol[c]) * push
    for c in range(4):
        ho[(c + 2) % 4] = fout[c] * l1[c, core]
        hi[(c + 2) % 4] = fin[c] * l1[c, 1 - core]


def total_push(core_ref, s0, got, k01, tt, a0, asum, tsum):
    for l in range(2):
        t2 = tt[l]
        t1 = tt[2 + l]
        s = s0[l] + got[l]
        mixed = s + (0.25 * t2 + t1) * a0[l] - (0.25 * H) * (k01[2 + l] * t2) * asum[2 + l]
        tsum[l] = t2 + t1 - H * (k01[l] * mixed)


def finish(core_ref, coef, p4, q4, l2, l1, hout, hin, k01, tt, vel, own, other):
    core = core_ref[0]
    co = Coef(coef)
    for c in range(4):
        dst = own if c < 2 else other
        for l in range(2):
            x = l1[c, l]
            l1s = q4[c, l] * (1.0 / 6.0) + co.vol[c] * (0.25 * tt[l] + tt[2 + l])
            rest = back(co, l1, vel, core, c, l) + (co.rate[c] * k01[l]) * (l1s - x)
            dst[c % 2, l] = (1.0 / 3.0) * p4[c, l] + 0.75 * l2[c, l] + x + H * rest
        dst[c % 2, core] = dst[c % 2, core] + H * hout[c]
        dst[c % 2, 1 - core] = dst[c % 2, 1 - core] + H * hin[c]


def assemble(core_ref, vol, own, other, tsum, tother, q, conc, dep):
    core = core_ref[0]
    for l in range(2):
        mine = 2 * core + l
        theirs = 2 * (1 - core) + l
        for c in range(2):
            conc[c, mine] = own[c, l]
            conc[c, theirs] = other[c, l]
            dep[c, mine] = q[c, mine] + vol[c] * tsum[l]
            dep[c, theirs] = q[c, theirs] + vol[c] * tother[l]


def call(body, outs, scalars, arrays, scratch=()):
    smem = pl.BlockSpec(memory_space=pltpu.SMEM)
    vmem = pl.BlockSpec(memory_space=pltpu.VMEM)
    size = sum(4 * a.size for a in arrays)
    return pl.pallas_call(
        body,
        out_shape=[jax.ShapeDtypeStruct(s, F32) for s in outs],
        in_specs=[smem] * len(scalars) + [vmem] * len(arrays),
        out_specs=[vmem] * len(outs),
        scratch_shapes=[pltpu.VMEM(s, F32) for s in scratch],
        compiler_params=pltpu.CompilerParams(vmem_limit_bytes=16 * 1024 * 1024),
        cost_estimate=pl.CostEstimate(flops=4 * size, bytes_accessed=size, transcendentals=0),
        name=body.__name__,
    )(*scalars, *arrays)


def shards(peers, conc, dep, velocity, label, dif, rate, vol, p, q):
    core = (lax.axis_index("size") % 2).astype(jnp.int32)[None]
    swap = [(0, 1), (1, 0), (2, 3), (3, 2)]
    far = [(0, 2), (2, 0), (1, 3), (3, 1)]
    face = []
    for g in range(peers - 1):
        for chip in (0, 2):
            a, b = (chip + 1) * peers + g, chip * peers + g + 1
            face += [(a, b), (b, a)]
    inner = lambda x: lax.ppermute(x, "size", swap)
    across = lambda x: lax.ppermute(x, "size", far)
    outer = lambda x: lax.ppermute(x, ("size", "gz"), face)
    field, four, pair, eight = (2, N, N), (4, N, N), (2, 2, N, N), (4, 2, N, N)

    (msg0,) = call(send_state, [(9, N, N)], (core, dif, rate, vol), (dep, conc))
    got0 = inner(msg0)
    (msg1,) = call(send_cot, [(10, N, N)], (core,), (p, q))
    got1 = inner(msg1)
    pk1, ho, c0, coef, u4, uin = call(
        sums_zero, [four, four, field, (16, N), eight, four], (core, dif, rate, vol), (dep, conc, got0)
    )
    gpk1 = across(pk1)
    hu0 = outer(ho)
    (abase,) = call(step_base, [eight], (core,), (coef, u4, uin, velocity))
    p4, q4, pbase, hop = call(
        cot_base, [eight, eight, eight, four], (core,), (coef, p, q, got1, velocity)
    )
    hp = outer(hop)
    a4, pk2 = call(sums_one, [eight, four], (core,), (coef, abase, hu0, velocity, c0))
    gpk2 = across(pk2)
    u1, ho1, hi1, k01, th, a0 = call(
        state_one,
        [eight, four, four, (6, N, N), four, field],
        (core,),
        (coef, pk1, gpk1, label, a4, u4),
    )
    hu1, iu1 = outer(ho1), inner(hi1)
    l2, ho2, hi2, s1, kk, asum = call(
        cot_two,
        [eight, four, four, field, field, four],
        (core,),
        (coef, pk2, gpk2, k01, th, p4, q4, pbase, hp, velocity, u1),
    )
    hl2, il2 = outer(ho2), inner(hi2)
    (pk3,) = call(
        sums_two,
        [four],
        (core,),
        (coef, u4, u1, hu1, iu1, k01, velocity, p4, q4, s1),
        scratch=[eight],
    )
    gpk3 = across(pk3)
    l1k, s0 = call(
        sums_three, [eight, field], (core,), (coef, l2, hl2, il2, k01, velocity, q4, u4)
    )
    gs0 = across(s0)
    l1, ho3, hi3, tt = call(
        cot_one, [eight, four, four, four], (core,), (coef, pk3, gpk3, k01, kk, asum, l1k, velocity)
    )
    hl1, il1 = outer(ho3), inner(hi3)
    (tsum,) = call(total_push, [field], (core,), (s0, gs0, k01, tt, a0, asum))
    tother = inner(tsum)
    own, other = call(
        finish, [pair, pair], (core,), (coef, p4, q4, l2, l1, hl1, il1, k01, tt, velocity)
    )
    theirs = inner(other)
    return tuple(
        call(assemble, [(2, 4, N, N), (2, 4, N, N)], (core, vol), (own, theirs, tsum, tother, q))
    )


def solution(mesh):
    state = P("size", "gz", None, None)
    flow = P("gz", None, None)
    in_specs = (state, state, flow, flow, P("size"), P("size"), P("size"), state, state)
    body = functools.partial(shards, mesh.shape["gz"])
    return jax.shard_map(
        body, mesh=mesh, in_specs=in_specs, out_specs=(state, state), check_vma=False
    )
```

```python
import functools

import jax
import jax.numpy as jnp
from jax import lax
from jax.experimental import pallas as pl
from jax.experimental.pallas import tpu as pltpu
from jax.sharding import PartitionSpec as P

H = 0.25
SURFACE_EFF = (0.1, 0.6, 1.2, 2.0)
N = 128
WORK = {
    "send_state": 0.0,
    "send_cot": 0.01,
    "sums_zero": 0.01,
    "sums_one": 0.01,
    "step_base": 0.01,
    "cot_base": 0.01,
    "state_one": 0.01,
    "state_two": 0.01,
    "sums_two": 0.01,
    "cot_two": 0.01,
    "cot_one_base": 0.01,
    "cot_one": 0.01,
    "sums_three": 0.01,
    "finish_base": 0.01,
    "finish": 0.01,
    "write_dep": 0.01,
    "write_conc": 0.01,
    "total_push": 0.01,
}
F32 = jnp.float32


def lateral(x):
    row = lax.broadcasted_iota(jnp.int32, x.shape, 0)
    col = lax.broadcasted_iota(jnp.int32, x.shape, 1)
    up = jnp.where(row > 0, pltpu.roll(x, 1, 0), 0.0)
    down = jnp.where(row < N - 1, pltpu.roll(x, N - 1, 0), 0.0)
    left = jnp.where(col > 0, pltpu.roll(x, 1, 1), 0.0)
    right = jnp.where(col < N - 1, pltpu.roll(x, N - 1, 1), 0.0)
    return (up + down) + (left + right) - 6.0 * x


def efficiency(label):
    out = jnp.zeros(label.shape, F32)
    for k in range(4):
        out = jnp.where(label == k, SURFACE_EFF[k], out)
    return out


class Coef:
    def __init__(self, ref):
        self.dif = [ref[c : c + 1, :] for c in range(4)]
        self.rate = [ref[4 + c : 5 + c, :] for c in range(4)]
        self.vol = [ref[8 + c : 9 + c, :] for c in range(4)]


def send_state(core_ref, dif, rate, vol, dep, conc, msg, mine, theta, rows):
    core = core_ref[0]
    other = 1 - core
    for l in range(2):
        msg[l] = vol[0] * dep[0, 2 * other + l] + vol[1] * dep[1, 2 * other + l]
        theta[l] = vol[0] * dep[0, 2 * core + l] + vol[1] * dep[1, 2 * core + l]
    for c in range(2):
        for l in range(2):
            msg[2 + 3 * c + l] = conc[c, 2 * other + l]
            mine[3 * c + l] = conc[c, 2 * core + l]
        msg[4 + 3 * c] = conc[c, 2 - other]
        mine[3 * c + 2] = conc[c, 2 - core]
    for k, ref in enumerate((dif, rate, vol)):
        for c in range(2):
            row = jnp.full((1, N), ref[c], F32)
            msg[8, 2 * k + c : 2 * k + c + 1, :] = row
            rows[2 * k + c : 2 * k + c + 1, :] = row


def send_cot(core_ref, p, q, msg):
    other = 1 - core_ref[0]
    for c in range(2):
        for l in range(2):
            msg[3 * c + l] = p[c, 2 * other + l]
            msg[6 + 2 * c + l] = q[c, 2 * other + l]
        msg[3 * c + 2] = p[c, 2 - other]


def sums_zero(core_ref, rows, theta, mine, got, pk1, ho, c0, coef, u4, uin):
    core = core_ref[0]
    for k in range(3):
        coef[4 * k : 4 * k + 2, :] = rows[2 * k : 2 * k + 2, :]
        coef[4 * k + 2 : 4 * k + 4, :] = got[8, 2 * k : 2 * k + 2, :]
    co = Coef(coef)
    for l in range(2):
        pk1[l] = got[l] + theta[l]
        total = jnp.zeros((N, N), F32)
        square = jnp.zeros((N, N), F32)
        for c in range(4):
            u = mine[3 * c + l] if c < 2 else got[2 + 3 * (c - 2) + l]
            u4[c, l] = u
            term = (co.vol[c] * co.rate[c]) * u
            total = total + term
            square = square + co.rate[c] * term
        pk1[2 + l] = total
        c0[l] = square
    for c in range(4):
        uin[c] = mine[3 * c + 2] if c < 2 else got[4 + 3 * (c - 2)]
        ho[(c + 2) % 4] = u4[c, core]


def advect(co, u4, vel, core, c, l):
    u = u4[c, l]
    out = co.dif[c] * lateral(u) - vel[2 * core + l] * u
    if l == 0:
        return out + co.dif[c] * u4[c, 1]
    return out + (co.dif[c] + vel[2 * core + 1]) * u4[c, 0]


def back(co, x4, vel, core, c, l):
    x = x4[c, l]
    out = co.dif[c] * lateral(x) - vel[2 * core + l] * x
    if l == 0:
        return out + (co.dif[c] + vel[2 * core + 1]) * x4[c, 1]
    return out + co.dif[c] * x4[c, 0]


def facing(co, vel, core):
    low = vel[2 * core]
    out_part = jnp.where(core == 0, low, 0.0)
    in_part = jnp.where(core == 1, low, 0.0)
    return (
        [co.dif[c] + out_part for c in range(4)],
        [co.dif[c] + in_part for c in range(4)],
    )


def step_base(core_ref, coef, u4, uin, vel, a4):
    core = core_ref[0]
    co = Coef(coef)
    _, fin = facing(co, vel, core)
    for c in range(4):
        for l in range(2):
            a4[c, l] = u4[c, l] + H * advect(co, u4, vel, core, c, l)
        a4[c, 1 - core] = a4[c, 1 - core] + H * (fin[c] * uin[c])


def cot_base(core_ref, coef, p, q, got, vel, p4, q4, base, ho):
    core = core_ref[0]
    co = Coef(coef)
    fout, _ = facing(co, vel, core)
    above = jnp.where(core == 0, vel[2 - core], 0.0)
    for c in range(4):
        for l in range(2):
            p4[c, l] = p[c, 2 * core + l] if c < 2 else got[3 * (c - 2) + l]
            q4[c, l] = q[c, 2 * core + l] if c < 2 else got[6 + 2 * (c - 2) + l]
        ho[(c + 2) % 4] = fout[c] * p4[c, core]
        for l in range(2):
            base[c, l] = back(co, p4, vel, core, c, l)
        pin = p[c, 2 - core] if c < 2 else got[3 * (c - 2) + 2]
        base[c, 1 - core] = base[c, 1 - core] + (co.dif[c] + above) * pin


def sums_one(core_ref, coef, base, hout, vel, c0, a4, pk2):
    core = core_ref[0]
    co = Coef(coef)
    fout, _ = facing(co, vel, core)
    for l in range(2):
        for c in range(4):
            a4[c, l] = base[c, l]
    for c in range(4):
        a4[c, core] = a4[c, core] + H * (fout[c] * hout[c])
    for l in range(2):
        total = jnp.zeros((N, N), F32)
        for c in range(4):
            total = total + (co.vol[c] * co.rate[c]) * a4[c, l]
        pk2[l] = total
        pk2[2 + l] = c0[l]


def state_one(core_ref, coef, pk1, got, label, a4, u4, u1, ho, hi, k01, th, a0s):
    core = core_ref[0]
    co = Coef(coef)
    for l in range(2):
        coll = efficiency(label[2 * core + l])
        theta = pk1[l] + got[l]
        a0 = pk1[2 + l] + got[2 + l]
        k0 = coll * jnp.exp(-theta)
        theta1 = theta + H * (k0 * a0)
        k01[l] = k0
        k01[2 + l] = coll * jnp.exp(-theta1)
        k01[4 + l] = coll
        th[l] = theta
        th[2 + l] = theta1
        a0s[l] = a0
        for c in range(4):
            u1[c, l] = a4[c, l] - (H * k0) * (co.rate[c] * u4[c, l])
    for c in range(4):
        ho[(c + 2) % 4] = u1[c, core]
        hi[(c + 2) % 4] = u1[c, 1 - core]


def state_two(core_ref, coef, u4, u1, hin, k01, vel, p4, q4, part, wout):
    core = core_ref[0]
    co = Coef(coef)
    fout, fin = facing(co, vel, core)
    for l in range(2):
        total = jnp.zeros((N, N), F32)
        for c in range(4):
            u = u1[c, l]
            rate = advect(co, u1, vel, core, c, l) - (co.rate[c] * k01[2 + l]) * u
            u2 = 0.75 * u4[c, l] + 0.25 * (u + H * rate)
            total = total + (co.rate[c] * (q4[c, l] - p4[c, l])) * u2
        part[l] = total
    edge = part[1 - core]
    for c in range(4):
        scaled = (0.25 * H) * co.rate[c]
        wout[c] = scaled * ((q4[c, core] - p4[c, core]) * fout[c])
        edge = edge + scaled * ((q4[c, 1 - core] - p4[c, 1 - core]) * (fin[c] * hin[c]))
    part[1 - core] = edge


def sums_two(core_ref, part, wout, hout, pk3):
    core = core_ref[0]
    edge = part[core]
    for c in range(4):
        edge = edge + wout[c] * hout[c]
    pk3[1 - core] = part[1 - core]
    pk3[core] = edge


def cot_two(core_ref, coef, pk2, got, k01, th, a0, p4, q4, base, hout, vel, l2, ho, hi, k2s, sums):
    core = core_ref[0]
    co = Coef(coef)
    fout, fin = facing(co, vel, core)
    for l in range(2):
        c0 = pk2[2 + l] + got[2 + l]
        a1 = (pk2[l] + got[l]) - (H * k01[l]) * c0
        theta2 = 0.75 * th[l] + 0.25 * (th[2 + l] + H * (k01[2 + l] * a1))
        k2 = k01[4 + l] * jnp.exp(-theta2)
        k2s[l] = k2
        sums[l] = a0[l]
        sums[2 + l] = a1
        sums[4 + l] = c0
        for c in range(4):
            p = p4[c, l]
            l2[c, l] = (2.0 / 3.0) * p + (2.0 / 3.0 * H) * (
                base[c, l] + (co.rate[c] * k2) * (q4[c, l] - p)
            )
    for c in range(4):
        l2[c, core] = l2[c, core] + (2.0 / 3.0 * H) * hout[c]
        ho[(c + 2) % 4] = fout[c] * l2[c, core]
        hi[(c + 2) % 4] = fin[c] * l2[c, 1 - core]


def cot_one_base(core_ref, coef, l2, hin, k01, vel, q4, u1, u4, l1, part):
    core = core_ref[0]
    co = Coef(coef)
    for c in range(4):
        for l in range(2):
            x = l2[c, l]
            w = (2.0 / 3.0) * q4[c, l] - x
            rest = back(co, l2, vel, core, c, l) + (co.rate[c] * k01[2 + l]) * w
            l1[c, l] = 0.25 * x + (0.25 * H) * rest
        l1[c, 1 - core] = l1[c, 1 - core] + (0.25 * H) * hin[c]
    for l in range(2):
        first = jnp.zeros((N, N), F32)
        zero = jnp.zeros((N, N), F32)
        for c in range(4):
            q = q4[c, l]
            first = first + (co.rate[c] * ((2.0 / 3.0) * q - l2[c, l])) * u1[c, l]
            zero = zero + (co.rate[c] * ((1.0 / 6.0) * q - l1[c, l])) * u4[c, l]
        part[l] = first
        part[2 + l] = zero


def cot_one(core_ref, coef, pk3, got, k01, k2s, sums, l1k, vel, l1, ho, hi, t2s):
    core = core_ref[0]
    co = Coef(coef)
    fout, fin = facing(co, vel, core)
    for l in range(2):
        t2 = (-2.0 / 3.0 * H) * k2s[l] * (pk3[l] + got[l])
        push = (0.25 * H) * (k01[2 + l] * t2)
        t2s[l] = t2
        t2s[2 + l] = sums[l]
        t2s[4 + l] = sums[2 + l]
        t2s[6 + l] = push * sums[4 + l]
        for c in range(4):
            l1[c, l] = l1k[c, l] + (co.rate[c] * co.vol[c]) * push
    for c in range(4):
        ho[(c + 2) % 4] = fout[c] * l1[c, core]
        hi[(c + 2) % 4] = fin[c] * l1[c, 1 - core]


def sums_three(core_ref, coef, base, part, hout, u4, l1, pk4):
    core = core_ref[0]
    co = Coef(coef)
    edge = part[2 + core]
    for c in range(4):
        more = (0.25 * H) * hout[c]
        l1[c, 1 - core] = base[c, 1 - core]
        l1[c, core] = base[c, core] + more
        edge = edge - (co.rate[c] * more) * u4[c, core]
    for l in range(2):
        pk4[l] = part[l]
    pk4[3 - core] = part[3 - core]
    pk4[2 + core] = edge


def total_push(core_ref, pk4, got, k01, t2s, tsum, mixed):
    for l in range(2):
        t2 = t2s[l]
        t1 = (-0.25 * H) * k01[2 + l] * ((pk4[l] + got[l]) + t2 * t2s[4 + l])
        both = 0.25 * t2 + t1
        zero = (pk4[2 + l] + got[2 + l]) + both * t2s[2 + l] - t2s[6 + l]
        tsum[l] = t2 + t1 - H * (k01[l] * zero)
        mixed[l] = both


def finish_base(core_ref, coef, p4, q4, l2, l1, hin, k01, mixed, vel, out):
    core = core_ref[0]
    co = Coef(coef)
    for l in range(2):
        for c in range(4):
            x = l1[c, l]
            l1s = q4[c, l] * (1.0 / 6.0) + co.vol[c] * mixed[l]
            rest = back(co, l1, vel, core, c, l) + (co.rate[c] * k01[l]) * (l1s - x)
            out[c, l] = (1.0 / 3.0) * p4[c, l] + 0.75 * l2[c, l] + x + H * rest
    for c in range(4):
        out[c, 1 - core] = out[c, 1 - core] + H * hin[c]


def finish(core_ref, base, hout, after, own, msg):
    core = core_ref[0]
    for c in range(4):
        dst = own if c < 2 else msg
        k = 2 * (c % 2)
        dst[k + 1 - core] = base[c, 1 - core]
        dst[k + core] = base[c, core] + H * hout[c]


def write_dep(core_ref, coef, tsum, got, q, dep, buf, sem):
    core = core_ref[0]
    vol = Coef(coef).vol
    copies = []
    for c in range(2):
        for k, (src, half) in enumerate(((tsum, core), (got, 1 - core))):
            for l in range(2):
                buf[c, 2 * half + l] = q[c, 2 * half + l] + vol[c] * src[l]
            there = pl.ds(2 * half, 2)
            copies.append(pltpu.make_async_copy(buf.at[c, there], dep.at[c, there], sem.at[2 * c + k]))
            copies[-1].start()
    for copy in copies:
        copy.wait()


def write_conc(core_ref, own, got, conc, sem):
    core = core_ref[0]
    copies = []
    for c in range(2):
        for k, (src, half) in enumerate(((own, core), (got, 1 - core))):
            copies.append(
                pltpu.make_async_copy(
                    src.at[pl.ds(2 * c, 2)], conc.at[c, pl.ds(2 * half, 2)], sem.at[2 * c + k]
                )
            )
            copies[-1].start()
    for copy in copies:
        copy.wait()


def call(body, outs, scalars, arrays, scratch=(), sems=0, hbm_out=False, size=None):
    smem = pl.BlockSpec(memory_space=pltpu.SMEM)
    vmem = pl.BlockSpec(memory_space=pltpu.VMEM)
    hbm = pl.BlockSpec(memory_space=pltpu.HBM)
    scratch_shapes = [pltpu.VMEM(s, F32) for s in scratch]
    if sems:
        scratch_shapes.append(pltpu.SemaphoreType.DMA((sems,)))
    if size is None:
        size = sum(4 * a.size for a in arrays)
    return pl.pallas_call(
        body,
        out_shape=[jax.ShapeDtypeStruct(s, F32) for s in outs],
        in_specs=[smem] * len(scalars) + [vmem] * len(arrays),
        out_specs=[hbm if hbm_out else vmem] * len(outs),
        scratch_shapes=scratch_shapes,
        compiler_params=pltpu.CompilerParams(vmem_limit_bytes=16 * 1024 * 1024),
        cost_estimate=pl.CostEstimate(
            flops=int(WORK[body.__name__] * 1e9), bytes_accessed=size, transcendentals=0
        ),
        name=body.__name__,
    )(*scalars, *arrays)


def shards(peers, conc, dep, velocity, label, dif, rate, vol, p, q):
    core = (lax.axis_index("size") % 2).astype(jnp.int32)[None]
    swap = [(0, 1), (1, 0), (2, 3), (3, 2)]
    far = [(0, 2), (2, 0), (1, 3), (3, 1)]
    face = []
    for g in range(peers - 1):
        for chip in (0, 2):
            a, b = (chip + 1) * peers + g, chip * peers + g + 1
            face += [(a, b), (b, a)]
    inner = lambda x: lax.ppermute(x, "size", swap)
    across = lambda x: lax.ppermute(x, "size", far)
    outer = lambda x: lax.ppermute(x, ("size", "gz"), face)
    layers = lambda n: (n, N, N)
    eight = (4, 2, N, N)

    msg0, mine, theta, rows = call(
        send_state,
        [layers(9), layers(6), layers(2), (8, N)],
        (core, dif, rate, vol),
        (dep, conc),
        size=0,
    )
    got0 = inner(msg0)
    (msg1,) = call(send_cot, [layers(10)], (core,), (p, q))
    got1 = inner(msg1)
    pk1, ho0, c0, coef, u4, uin = call(
        sums_zero,
        [layers(4), layers(4), layers(2), (16, N), eight, layers(4)],
        (core,),
        (rows, theta, mine, got0),
    )
    gpk1 = across(pk1)
    hu0 = outer(ho0)
    (abase,) = call(step_base, [eight], (core,), (coef, u4, uin, velocity))
    p4, q4, pbase, hop = call(
        cot_base, [eight, eight, eight, layers(4)], (core,), (coef, p, q, got1, velocity)
    )
    hp = outer(hop)
    a4, pk2 = call(sums_one, [eight, layers(4)], (core,), (coef, abase, hu0, velocity, c0))
    gpk2 = across(pk2)
    u1, ho1, hi1, k01, th, a0 = call(
        state_one,
        [eight, layers(4), layers(4), layers(6), layers(4), layers(2)],
        (core,),
        (coef, pk1, gpk1, label, a4, u4),
    )
    iu1 = inner(hi1)
    hu1 = outer(ho1)
    part2, wout = call(
        state_two, [layers(2), layers(4)], (core,), (coef, u4, u1, iu1, k01, velocity, p4, q4)
    )
    l2, ho2, hi2, k2s, sums = call(
        cot_two,
        [eight, layers(4), layers(4), layers(2), layers(6)],
        (core,),
        (coef, pk2, gpk2, k01, th, a0, p4, q4, pbase, hp, velocity),
    )
    il2 = inner(hi2)
    hl2 = outer(ho2)
    (pk3,) = call(sums_two, [layers(2)], (core,), (part2, wout, hu1))
    gpk3 = across(pk3)
    l1base, part1 = call(
        cot_one_base, [eight, layers(4)], (core,), (coef, l2, il2, k01, velocity, q4, u1, u4)
    )
    l1k, pk4 = call(sums_three, [eight, layers(4)], (core,), (coef, l1base, part1, hl2, u4))
    gpk4 = across(pk4)
    l1, ho3, hi3, t2s = call(
        cot_one,
        [eight, layers(4), layers(4), layers(8)],
        (core,),
        (coef, pk3, gpk3, k01, k2s, sums, l1k, velocity),
    )
    il1 = inner(hi3)
    hl1 = outer(ho3)
    tsum, mixed = call(
        total_push, [layers(2), layers(2)], (core,), (pk4, gpk4, k01, t2s)
    )
    tother = inner(tsum)
    (base,) = call(
        finish_base, [eight], (core,), (coef, p4, q4, l2, l1, il1, k01, mixed, velocity)
    )
    own, msg = call(finish, [layers(4), layers(4)], (core,), (base, hl1, tother))
    theirs = inner(msg)
    state = (2, 4, N, N)
    (dep_out,) = call(
        write_dep, [state], (core,), (coef, tsum, tother, q), [state], 4, hbm_out=True
    )
    (conc_out,) = call(write_conc, [state], (core,), (own, theirs), (), 4, hbm_out=True)
    return conc_out, dep_out


def solution(mesh):
    state = P("size", "gz", None, None)
    flow = P("gz", None, None)
    in_specs = (state, state, flow, flow, P("size"), P("size"), P("size"), state, state)
    body = functools.partial(shards, mesh.shape["gz"])
    return jax.shard_map(
        body, mesh=mesh, in_specs=in_specs, out_specs=(state, state), check_vma=False
    )
```

```python
import functools

import jax
import jax.numpy as jnp
from jax import lax
from jax.experimental import pallas as pl
from jax.experimental.pallas import tpu as pltpu
from jax.sharding import PartitionSpec as P

H = 0.25
SURFACE_EFF = (0.1, 0.6, 1.2, 2.0)
N = 128
WORK = {
    "send_state": 0.01,
    "send_cot": 0.01,
    "sums_zero": 0.01,
    "sums_one": 0.01,
    "step_base": 0.01,
    "cot_base": 0.01,
    "state_one": 0.01,
    "state_two": 0.01,
    "sums_two": 0.01,
    "cot_two": 0.01,
    "cot_one_base": 0.01,
    "cot_one": 0.01,
    "sums_three": 0.01,
    "finish_base": 0.01,
    "finish": 0.01,
    "write_dep": 0.01,
    "write_conc": 0.01,
    "total_push": 0.01,
    "kappa_zero": 2.0,
    "cot_start": 3.0,
}
F32 = jnp.float32


def lateral(x):
    row = lax.broadcasted_iota(jnp.int32, x.shape, 0)
    col = lax.broadcasted_iota(jnp.int32, x.shape, 1)
    up = jnp.where(row > 0, pltpu.roll(x, 1, 0), 0.0)
    down = jnp.where(row < N - 1, pltpu.roll(x, N - 1, 0), 0.0)
    left = jnp.where(col > 0, pltpu.roll(x, 1, 1), 0.0)
    right = jnp.where(col < N - 1, pltpu.roll(x, N - 1, 1), 0.0)
    return (up + down) + (left + right) - 6.0 * x


def efficiency(label):
    out = jnp.zeros(label.shape, F32)
    for k in range(4):
        out = jnp.where(label == k, SURFACE_EFF[k], out)
    return out


class Coef:
    def __init__(self, ref):
        self.dif = [ref[c : c + 1, :] for c in range(4)]
        self.rate = [ref[4 + c : 5 + c, :] for c in range(4)]
        self.vol = [ref[8 + c : 9 + c, :] for c in range(4)]


def send_state(core_ref, dif, rate, vol, dep, conc, msg, mine, theta, rows):
    core = core_ref[0]
    other = 1 - core
    for l in range(2):
        msg[l] = vol[0] * dep[0, 2 * other + l] + vol[1] * dep[1, 2 * other + l]
        theta[l] = vol[0] * dep[0, 2 * core + l] + vol[1] * dep[1, 2 * core + l]
    for c in range(2):
        for l in range(2):
            msg[2 + 3 * c + l] = conc[c, 2 * other + l]
            mine[3 * c + l] = conc[c, 2 * core + l]
        msg[4 + 3 * c] = conc[c, 2 - other]
        mine[3 * c + 2] = conc[c, 2 - core]
    for k, ref in enumerate((dif, rate, vol)):
        for c in range(2):
            row = jnp.full((1, N), ref[c], F32)
            msg[8, 2 * k + c : 2 * k + c + 1, :] = row
            rows[2 * k + c : 2 * k + c + 1, :] = row


def send_cot(core_ref, p, q, msg):
    other = 1 - core_ref[0]
    for c in range(2):
        for l in range(2):
            msg[3 * c + l] = p[c, 2 * other + l]
            msg[6 + 2 * c + l] = q[c, 2 * other + l]
        msg[3 * c + 2] = p[c, 2 - other]


def sums_zero(core_ref, rows, theta, mine, got, pk1, ho, sums, coef, u4, uin):
    core = core_ref[0]
    for k in range(3):
        coef[4 * k : 4 * k + 2, :] = rows[2 * k : 2 * k + 2, :]
        coef[4 * k + 2 : 4 * k + 4, :] = got[8, 2 * k : 2 * k + 2, :]
    co = Coef(coef)
    for l in range(2):
        pk1[l] = got[l] + theta[l]
        total = jnp.zeros((N, N), F32)
        square = jnp.zeros((N, N), F32)
        for c in range(4):
            u = mine[3 * c + l] if c < 2 else got[2 + 3 * (c - 2) + l]
            u4[c, l] = u
            term = (co.vol[c] * co.rate[c]) * u
            total = total + term
            square = square + co.rate[c] * term
        sums[l] = total
        sums[2 + l] = square
    for c in range(4):
        uin[c] = mine[3 * c + 2] if c < 2 else got[4 + 3 * (c - 2)]
        ho[(c + 2) % 4] = u4[c, core]


def advect(co, u4, vel, core, c, l):
    u = u4[c, l]
    out = co.dif[c] * lateral(u) - vel[2 * core + l] * u
    if l == 0:
        return out + co.dif[c] * u4[c, 1]
    return out + (co.dif[c] + vel[2 * core + 1]) * u4[c, 0]


def back(co, x4, vel, core, c, l):
    x = x4[c, l]
    out = co.dif[c] * lateral(x) - vel[2 * core + l] * x
    if l == 0:
        return out + (co.dif[c] + vel[2 * core + 1]) * x4[c, 1]
    return out + co.dif[c] * x4[c, 0]


def facing(co, vel, core):
    low = vel[2 * core]
    out_part = jnp.where(core == 0, low, 0.0)
    in_part = jnp.where(core == 1, low, 0.0)
    return (
        [co.dif[c] + out_part for c in range(4)],
        [co.dif[c] + in_part for c in range(4)],
    )


def step_base(core_ref, coef, u4, uin, vel, a4):
    core = core_ref[0]
    co = Coef(coef)
    _, fin = facing(co, vel, core)
    for c in range(4):
        for l in range(2):
            a4[c, l] = u4[c, l] + H * advect(co, u4, vel, core, c, l)
        a4[c, 1 - core] = a4[c, 1 - core] + H * (fin[c] * uin[c])


def cot_base(core_ref, coef, p, q, got, vel, p4, q4, base, ho):
    core = core_ref[0]
    co = Coef(coef)
    fout, _ = facing(co, vel, core)
    above = jnp.where(core == 0, vel[2 - core], 0.0)
    for c in range(4):
        for l in range(2):
            p4[c, l] = p[c, 2 * core + l] if c < 2 else got[3 * (c - 2) + l]
            q4[c, l] = q[c, 2 * core + l] if c < 2 else got[6 + 2 * (c - 2) + l]
        ho[(c + 2) % 4] = fout[c] * p4[c, core]
        for l in range(2):
            base[c, l] = back(co, p4, vel, core, c, l)
        pin = p[c, 2 - core] if c < 2 else got[3 * (c - 2) + 2]
        base[c, 1 - core] = base[c, 1 - core] + (co.dif[c] + above) * pin


def kappa_zero(core_ref, pk1, got, label, k0s, th):
    core = core_ref[0]
    for l in range(2):
        coll = efficiency(label[2 * core + l])
        theta = pk1[l] + got[l]
        k0s[l] = coll * jnp.exp(-theta)
        k0s[2 + l] = coll
        th[l] = theta


def state_one(core_ref, coef, base, hout, vel, sums, k0s, u4, after, u1, ho, hi, pk2):
    core = core_ref[0]
    co = Coef(coef)
    fout, _ = facing(co, vel, core)
    halo = [H * (fout[c] * hout[c]) for c in range(4)]
    extra = jnp.zeros((N, N), F32)
    for c in range(4):
        extra = extra + (co.vol[c] * co.rate[c]) * halo[c]
    for l in range(2):
        total = jnp.zeros((N, N), F32)
        for c in range(4):
            a = base[c, l]
            total = total + (co.vol[c] * co.rate[c]) * a
            u1[c, l] = a - (H * k0s[l]) * (co.rate[c] * u4[c, l])
        pk2[l] = total
        pk2[2 + l] = sums[2 + l]
        pk2[4 + l] = sums[l]
    pk2[core] = pk2[core] + extra
    for c in range(4):
        edge = u1[c, core] + halo[c]
        u1[c, core] = edge
        ho[(c + 2) % 4] = edge
        hi[(c + 2) % 4] = u1[c, 1 - core]


def state_two(core_ref, coef, u4, u1, hin, vel, p4, q4, part, wout):
    core = core_ref[0]
    co = Coef(coef)
    fout, fin = facing(co, vel, core)
    for l in range(2):
        total = jnp.zeros((N, N), F32)
        react = jnp.zeros((N, N), F32)
        for c in range(4):
            u = u1[c, l]
            w = co.rate[c] * (q4[c, l] - p4[c, l])
            total = total + w * (0.75 * u4[c, l] + 0.25 * (u + H * advect(co, u1, vel, core, c, l)))
            react = react + (0.25 * H) * (w * (co.rate[c] * u))
        part[l] = total
        part[2 + l] = react
    edge = part[1 - core]
    for c in range(4):
        scaled = (0.25 * H) * co.rate[c]
        wout[c] = scaled * ((q4[c, core] - p4[c, core]) * fout[c])
        edge = edge + scaled * ((q4[c, 1 - core] - p4[c, 1 - core]) * (fin[c] * hin[c]))
    part[1 - core] = edge


def sums_two(core_ref, part, wout, hout, k01, pk3):
    core = core_ref[0]
    for l in range(2):
        pk3[l] = part[l] - k01[2 + l] * part[2 + l]
    edge = pk3[core]
    for c in range(4):
        edge = edge + wout[c] * hout[c]
    pk3[core] = edge


def cot_start(core_ref, p4, base, hout, start):
    core = core_ref[0]
    for c in range(4):
        for l in range(2):
            start[c, l] = (2.0 / 3.0) * p4[c, l] + (2.0 / 3.0 * H) * base[c, l]
        start[c, core] = start[c, core] + (2.0 / 3.0 * H) * hout[c]


def cot_two(core_ref, coef, pk2, got, k0s, th, p4, q4, base, vel, l2, ho, hi, k01, k2s, sums):
    core = core_ref[0]
    co = Coef(coef)
    fout, fin = facing(co, vel, core)
    for l in range(2):
        k0 = k0s[l]
        a0 = pk2[4 + l] + got[4 + l]
        c0 = pk2[2 + l] + got[2 + l]
        theta1 = th[l] + H * (k0 * a0)
        k1 = k0s[2 + l] * jnp.exp(-theta1)
        k01[l] = k0
        k01[2 + l] = k1
        a1 = (pk2[l] + got[l]) - (H * k0) * c0
        theta2 = 0.75 * th[l] + 0.25 * (theta1 + H * (k1 * a1))
        k2 = k0s[2 + l] * jnp.exp(-theta2)
        k2s[l] = k2
        sums[l] = a0
        sums[2 + l] = a1
        sums[4 + l] = c0
        for c in range(4):
            p = p4[c, l]
            l2[c, l] = base[c, l] + (2.0 / 3.0 * H) * ((co.rate[c] * k2) * (q4[c, l] - p))
    for c in range(4):
        ho[(c + 2) % 4] = fout[c] * l2[c, core]
        hi[(c + 2) % 4] = fin[c] * l2[c, 1 - core]


def cot_one_base(core_ref, coef, l2, hin, k01, vel, q4, u1, u4, l1, part):
    core = core_ref[0]
    co = Coef(coef)
    for c in range(4):
        for l in range(2):
            x = l2[c, l]
            w = (2.0 / 3.0) * q4[c, l] - x
            rest = back(co, l2, vel, core, c, l) + (co.rate[c] * k01[2 + l]) * w
            l1[c, l] = 0.25 * x + (0.25 * H) * rest
        l1[c, 1 - core] = l1[c, 1 - core] + (0.25 * H) * hin[c]
    for l in range(2):
        first = jnp.zeros((N, N), F32)
        zero = jnp.zeros((N, N), F32)
        for c in range(4):
            q = q4[c, l]
            first = first + (co.rate[c] * ((2.0 / 3.0) * q - l2[c, l])) * u1[c, l]
            zero = zero + (co.rate[c] * ((1.0 / 6.0) * q - l1[c, l])) * u4[c, l]
        part[l] = first
        part[2 + l] = zero


def cot_one(core_ref, coef, pk3, got, k01, k2s, sums, l1k, vel, l1, ho, hi, t2s):
    core = core_ref[0]
    co = Coef(coef)
    fout, fin = facing(co, vel, core)
    for l in range(2):
        t2 = (-2.0 / 3.0 * H) * k2s[l] * (pk3[l] + got[l])
        push = (0.25 * H) * (k01[2 + l] * t2)
        t2s[l] = t2
        t2s[2 + l] = sums[l]
        t2s[4 + l] = sums[2 + l]
        t2s[6 + l] = push * sums[4 + l]
        for c in range(4):
            l1[c, l] = l1k[c, l] + (co.rate[c] * co.vol[c]) * push
    for c in range(4):
        ho[(c + 2) % 4] = fout[c] * l1[c, core]
        hi[(c + 2) % 4] = fin[c] * l1[c, 1 - core]


def sums_three(core_ref, coef, base, part, hout, u4, l1, pk4):
    core = core_ref[0]
    co = Coef(coef)
    edge = part[2 + core]
    for c in range(4):
        more = (0.25 * H) * hout[c]
        l1[c, 1 - core] = base[c, 1 - core]
        l1[c, core] = base[c, core] + more
        edge = edge - (co.rate[c] * more) * u4[c, core]
    for l in range(2):
        pk4[l] = part[l]
    pk4[3 - core] = part[3 - core]
    pk4[2 + core] = edge


def total_push(core_ref, pk4, got, k01, t2s, tsum, mixed):
    for l in range(2):
        t2 = t2s[l]
        t1 = (-0.25 * H) * k01[2 + l] * ((pk4[l] + got[l]) + t2 * t2s[4 + l])
        both = 0.25 * t2 + t1
        zero = (pk4[2 + l] + got[2 + l]) + both * t2s[2 + l] - t2s[6 + l]
        tsum[l] = t2 + t1 - H * (k01[l] * zero)
        mixed[l] = both


def finish_base(core_ref, coef, p4, q4, l2, l1, hin, k01, mixed, vel, out):
    core = core_ref[0]
    co = Coef(coef)
    for l in range(2):
        for c in range(4):
            x = l1[c, l]
            l1s = q4[c, l] * (1.0 / 6.0) + co.vol[c] * mixed[l]
            rest = back(co, l1, vel, core, c, l) + (co.rate[c] * k01[l]) * (l1s - x)
            out[c, l] = (1.0 / 3.0) * p4[c, l] + 0.75 * l2[c, l] + x + H * rest
    for c in range(4):
        out[c, 1 - core] = out[c, 1 - core] + H * hin[c]


def finish(core_ref, base, hout, after, own, msg):
    core = core_ref[0]
    for c in range(4):
        dst = own if c < 2 else msg
        k = 2 * (c % 2)
        dst[k + 1 - core] = base[c, 1 - core]
        dst[k + core] = base[c, core] + H * hout[c]


def write_dep(core_ref, coef, tsum, got, q, dep, buf, sem):
    core = core_ref[0]
    vol = Coef(coef).vol
    copies = []
    for c in range(2):
        for k, (src, half) in enumerate(((tsum, core), (got, 1 - core))):
            for l in range(2):
                buf[c, 2 * half + l] = q[c, 2 * half + l] + vol[c] * src[l]
            there = pl.ds(2 * half, 2)
            copies.append(pltpu.make_async_copy(buf.at[c, there], dep.at[c, there], sem.at[2 * c + k]))
            copies[-1].start()
    for copy in copies:
        copy.wait()


def write_conc(core_ref, own, got, conc, sem):
    core = core_ref[0]
    copies = []
    for c in range(2):
        for k, (src, half) in enumerate(((own, core), (got, 1 - core))):
            copies.append(
                pltpu.make_async_copy(
                    src.at[pl.ds(2 * c, 2)], conc.at[c, pl.ds(2 * half, 2)], sem.at[2 * c + k]
                )
            )
            copies[-1].start()
    for copy in copies:
        copy.wait()


def call(body, outs, scalars, arrays, scratch=(), sems=0, hbm_out=False, size=None):
    smem = pl.BlockSpec(memory_space=pltpu.SMEM)
    vmem = pl.BlockSpec(memory_space=pltpu.VMEM)
    hbm = pl.BlockSpec(memory_space=pltpu.HBM)
    scratch_shapes = [pltpu.VMEM(s, F32) for s in scratch]
    if sems:
        scratch_shapes.append(pltpu.SemaphoreType.DMA((sems,)))
    if size is None:
        size = sum(4 * a.size for a in arrays)
    return pl.pallas_call(
        body,
        out_shape=[jax.ShapeDtypeStruct(s, F32) for s in outs],
        in_specs=[smem] * len(scalars) + [vmem] * len(arrays),
        out_specs=[hbm if hbm_out else vmem] * len(outs),
        scratch_shapes=scratch_shapes,
        compiler_params=pltpu.CompilerParams(vmem_limit_bytes=16 * 1024 * 1024),
        cost_estimate=pl.CostEstimate(
            flops=int(WORK[body.__name__] * 1e9), bytes_accessed=size, transcendentals=0
        ),
        name=body.__name__,
    )(*scalars, *arrays)


def shards(peers, conc, dep, velocity, label, dif, rate, vol, p, q):
    core = (lax.axis_index("size") % 2).astype(jnp.int32)[None]
    swap = [(0, 1), (1, 0), (2, 3), (3, 2)]
    far = [(0, 2), (2, 0), (1, 3), (3, 1)]
    face = []
    for g in range(peers - 1):
        for chip in (0, 2):
            a, b = (chip + 1) * peers + g, chip * peers + g + 1
            face += [(a, b), (b, a)]
    inner = lambda x: lax.ppermute(x, "size", swap)
    across = lambda x: lax.ppermute(x, "size", far)
    outer = lambda x: lax.ppermute(x, ("size", "gz"), face)
    layers = lambda n: (n, N, N)
    eight = (4, 2, N, N)

    msg0, mine, theta, rows = call(
        send_state,
        [layers(9), layers(6), layers(2), (8, N)],
        (core, dif, rate, vol),
        (dep, conc),
        size=0,
    )
    got0 = inner(msg0)
    (msg1,) = call(send_cot, [layers(10)], (core,), (p, q))
    got1 = inner(msg1)
    pk1, ho0, csums, coef, u4, uin = call(
        sums_zero,
        [layers(2), layers(4), layers(4), (16, N), eight, layers(4)],
        (core,),
        (rows, theta, mine, got0),
    )
    gpk1 = across(pk1)
    hu0 = outer(ho0)
    (abase,) = call(step_base, [eight], (core,), (coef, u4, uin, velocity))
    p4, q4, pbase, hop = call(
        cot_base, [eight, eight, eight, layers(4)], (core,), (coef, p, q, got1, velocity)
    )
    hp = outer(hop)
    k0s, th = call(kappa_zero, [layers(4), layers(2)], (core,), (pk1, gpk1, label))
    u1, ho1, hi1, pk2 = call(
        state_one,
        [eight, layers(4), layers(4), layers(6)],
        (core,),
        (coef, abase, hu0, velocity, csums, k0s, u4, pbase),
    )
    gpk2 = across(pk2)
    iu1 = inner(hi1)
    hu1 = outer(ho1)
    part2, wout = call(
        state_two, [layers(4), layers(4)], (core,), (coef, u4, u1, iu1, velocity, p4, q4)
    )
    (l2start,) = call(cot_start, [eight], (core,), (p4, pbase, hp))
    l2, ho2, hi2, k01, k2s, sums = call(
        cot_two,
        [eight, layers(4), layers(4), layers(4), layers(2), layers(6)],
        (core,),
        (coef, pk2, gpk2, k0s, th, p4, q4, l2start, velocity),
    )
    il2 = inner(hi2)
    hl2 = outer(ho2)
    (pk3,) = call(sums_two, [layers(2)], (core,), (part2, wout, hu1, k01))
    gpk3 = across(pk3)
    l1base, part1 = call(
        cot_one_base, [eight, layers(4)], (core,), (coef, l2, il2, k01, velocity, q4, u1, u4)
    )
    l1k, pk4 = call(sums_three, [eight, layers(4)], (core,), (coef, l1base, part1, hl2, u4))
    gpk4 = across(pk4)
    l1, ho3, hi3, t2s = call(
        cot_one,
        [eight, layers(4), layers(4), layers(8)],
        (core,),
        (coef, pk3, gpk3, k01, k2s, sums, l1k, velocity),
    )
    il1 = inner(hi3)
    hl1 = outer(ho3)
    tsum, mixed = call(
        total_push, [layers(2), layers(2)], (core,), (pk4, gpk4, k01, t2s)
    )
    tother = inner(tsum)
    (base,) = call(
        finish_base, [eight], (core,), (coef, p4, q4, l2, l1, il1, k01, mixed, velocity)
    )
    own, msg = call(finish, [layers(4), layers(4)], (core,), (base, hl1, tother))
    theirs = inner(msg)
    state = (2, 4, N, N)
    (dep_out,) = call(
        write_dep, [state], (core,), (coef, tsum, tother, q), [state], 4, hbm_out=True
    )
    (conc_out,) = call(write_conc, [state], (core,), (own, theirs), (), 4, hbm_out=True)
    return conc_out, dep_out


def solution(mesh):
    state = P("size", "gz", None, None)
    flow = P("gz", None, None)
    in_specs = (state, state, flow, flow, P("size"), P("size"), P("size"), state, state)
    body = functools.partial(shards, mesh.shape["gz"])
    return jax.shard_map(
        body, mesh=mesh, in_specs=in_specs, out_specs=(state, state), check_vma=False
    )
```

```python
import functools

import jax
import jax.numpy as jnp
from jax import lax
from jax.experimental import pallas as pl
from jax.experimental.pallas import tpu as pltpu
from jax.sharding import PartitionSpec as P

H = 0.25
SURFACE_EFF = (0.1, 0.6, 1.2, 2.0)
N = 128
WORK = {
    "send_state": 0.01,
    "send_cot": 0.01,
    "sums_zero": 0.01,
    "sums_one": 0.01,
    "step_base": 0.01,
    "cot_base": 0.01,
    "state_one": 0.01,
    "state_two": 0.01,
    "sums_two": 0.01,
    "cot_two": 0.01,
    "cot_one_base": 0.01,
    "cot_one": 2.0,
    "sums_three": 0.01,
    "finish_base": 0.01,
    "finish": 0.01,
    "write_dep": 0.01,
    "write_conc": 0.01,
    "total_push": 0.01,
    "kappa_zero": 2.0,
    "cot_start": 3.0,
}
F32 = jnp.float32


def lateral(x):
    row = lax.broadcasted_iota(jnp.int32, x.shape, 0)
    col = lax.broadcasted_iota(jnp.int32, x.shape, 1)
    up = jnp.where(row > 0, pltpu.roll(x, 1, 0), 0.0)
    down = jnp.where(row < N - 1, pltpu.roll(x, N - 1, 0), 0.0)
    left = jnp.where(col > 0, pltpu.roll(x, 1, 1), 0.0)
    right = jnp.where(col < N - 1, pltpu.roll(x, N - 1, 1), 0.0)
    return (up + down) + (left + right) - 6.0 * x


def efficiency(label):
    out = jnp.zeros(label.shape, F32)
    for k in range(4):
        out = jnp.where(label == k, SURFACE_EFF[k], out)
    return out


class Coef:
    def __init__(self, ref):
        self.dif = [ref[c : c + 1, :] for c in range(4)]
        self.rate = [ref[4 + c : 5 + c, :] for c in range(4)]
        self.vol = [ref[8 + c : 9 + c, :] for c in range(4)]


def send_state(core_ref, dif, rate, vol, dep, conc, msg, mine, theta, rows):
    core = core_ref[0]
    other = 1 - core
    for l in range(2):
        msg[l] = vol[0] * dep[0, 2 * other + l] + vol[1] * dep[1, 2 * other + l]
        theta[l] = vol[0] * dep[0, 2 * core + l] + vol[1] * dep[1, 2 * core + l]
    for c in range(2):
        for l in range(2):
            msg[2 + 3 * c + l] = conc[c, 2 * other + l]
            mine[3 * c + l] = conc[c, 2 * core + l]
        msg[4 + 3 * c] = conc[c, 2 - other]
        mine[3 * c + 2] = conc[c, 2 - core]
    for k, ref in enumerate((dif, rate, vol)):
        for c in range(2):
            row = jnp.full((1, N), ref[c], F32)
            msg[8, 2 * k + c : 2 * k + c + 1, :] = row
            rows[2 * k + c : 2 * k + c + 1, :] = row


def send_cot(core_ref, p, q, msg):
    other = 1 - core_ref[0]
    for c in range(2):
        for l in range(2):
            msg[3 * c + l] = p[c, 2 * other + l]
            msg[6 + 2 * c + l] = q[c, 2 * other + l]
        msg[3 * c + 2] = p[c, 2 - other]


def sums_zero(core_ref, rows, theta, mine, got, pk1, ho, sums, coef, u4, uin):
    core = core_ref[0]
    for k in range(3):
        coef[4 * k : 4 * k + 2, :] = rows[2 * k : 2 * k + 2, :]
        coef[4 * k + 2 : 4 * k + 4, :] = got[8, 2 * k : 2 * k + 2, :]
    co = Coef(coef)
    for l in range(2):
        pk1[l] = got[l] + theta[l]
        total = jnp.zeros((N, N), F32)
        square = jnp.zeros((N, N), F32)
        for c in range(4):
            u = mine[3 * c + l] if c < 2 else got[2 + 3 * (c - 2) + l]
            u4[c, l] = u
            term = (co.vol[c] * co.rate[c]) * u
            total = total + term
            square = square + co.rate[c] * term
        sums[l] = total
        sums[2 + l] = square
    for c in range(4):
        uin[c] = mine[3 * c + 2] if c < 2 else got[4 + 3 * (c - 2)]
        ho[(c + 2) % 4] = u4[c, core]


def advect(co, u4, vel, core, c, l):
    u = u4[c, l]
    out = co.dif[c] * lateral(u) - vel[2 * core + l] * u
    if l == 0:
        return out + co.dif[c] * u4[c, 1]
    return out + (co.dif[c] + vel[2 * core + 1]) * u4[c, 0]


def back(co, x4, vel, core, c, l):
    x = x4[c, l]
    out = co.dif[c] * lateral(x) - vel[2 * core + l] * x
    if l == 0:
        return out + (co.dif[c] + vel[2 * core + 1]) * x4[c, 1]
    return out + co.dif[c] * x4[c, 0]


def facing(co, vel, core):
    low = vel[2 * core]
    out_part = jnp.where(core == 0, low, 0.0)
    in_part = jnp.where(core == 1, low, 0.0)
    return (
        [co.dif[c] + out_part for c in range(4)],
        [co.dif[c] + in_part for c in range(4)],
    )


def step_base(core_ref, coef, u4, uin, vel, a4):
    core = core_ref[0]
    co = Coef(coef)
    _, fin = facing(co, vel, core)
    for c in range(4):
        for l in range(2):
            a4[c, l] = u4[c, l] + H * advect(co, u4, vel, core, c, l)
        a4[c, 1 - core] = a4[c, 1 - core] + H * (fin[c] * uin[c])


def cot_base(core_ref, coef, p, q, got, vel, p4, q4, base, ho):
    core = core_ref[0]
    co = Coef(coef)
    fout, _ = facing(co, vel, core)
    above = jnp.where(core == 0, vel[2 - core], 0.0)
    for c in range(4):
        for l in range(2):
            p4[c, l] = p[c, 2 * core + l] if c < 2 else got[3 * (c - 2) + l]
            q4[c, l] = q[c, 2 * core + l] if c < 2 else got[6 + 2 * (c - 2) + l]
        ho[(c + 2) % 4] = fout[c] * p4[c, core]
        for l in range(2):
            base[c, l] = back(co, p4, vel, core, c, l)
        pin = p[c, 2 - core] if c < 2 else got[3 * (c - 2) + 2]
        base[c, 1 - core] = base[c, 1 - core] + (co.dif[c] + above) * pin


def kappa_zero(core_ref, pk1, got, label, k0s, th):
    core = core_ref[0]
    for l in range(2):
        coll = efficiency(label[2 * core + l])
        theta = pk1[l] + got[l]
        k0s[l] = coll * jnp.exp(-theta)
        k0s[2 + l] = coll
        th[l] = theta


def state_one(core_ref, coef, base, hout, vel, sums, k0s, u4, after, u1, ho, hi, pk2):
    core = core_ref[0]
    co = Coef(coef)
    fout, _ = facing(co, vel, core)
    halo = [H * (fout[c] * hout[c]) for c in range(4)]
    extra = jnp.zeros((N, N), F32)
    for c in range(4):
        extra = extra + (co.vol[c] * co.rate[c]) * halo[c]
    for l in range(2):
        total = jnp.zeros((N, N), F32)
        for c in range(4):
            u = base[c, l] - (H * k0s[l]) * (co.rate[c] * u4[c, l])
            total = total + (co.vol[c] * co.rate[c]) * u
            u1[c, l] = u
        pk2[l] = total
        pk2[2 + l] = sums[l]
    pk2[core] = pk2[core] + extra
    for c in range(4):
        edge = u1[c, core] + halo[c]
        u1[c, core] = edge
        ho[(c + 2) % 4] = edge
        hi[(c + 2) % 4] = u1[c, 1 - core]


def state_two(core_ref, coef, u4, u1, hin, vel, p4, q4, part, wout):
    core = core_ref[0]
    co = Coef(coef)
    fout, fin = facing(co, vel, core)
    for l in range(2):
        total = jnp.zeros((N, N), F32)
        react = jnp.zeros((N, N), F32)
        for c in range(4):
            u = u1[c, l]
            w = co.rate[c] * (q4[c, l] - p4[c, l])
            total = total + w * (0.75 * u4[c, l] + 0.25 * (u + H * advect(co, u1, vel, core, c, l)))
            react = react + (0.25 * H) * (w * (co.rate[c] * u))
        part[l] = total
        part[2 + l] = react
    edge = part[1 - core]
    for c in range(4):
        scaled = (0.25 * H) * co.rate[c]
        wout[c] = scaled * ((q4[c, core] - p4[c, core]) * fout[c])
        edge = edge + scaled * ((q4[c, 1 - core] - p4[c, 1 - core]) * (fin[c] * hin[c]))
    part[1 - core] = edge


def sums_two(core_ref, part, wout, hout, k01, pk3):
    core = core_ref[0]
    for l in range(2):
        pk3[l] = part[l] - k01[2 + l] * part[2 + l]
    edge = pk3[core]
    for c in range(4):
        edge = edge + wout[c] * hout[c]
    pk3[core] = edge


def cot_start(core_ref, p4, base, hout, start):
    core = core_ref[0]
    for c in range(4):
        for l in range(2):
            start[c, l] = (2.0 / 3.0) * p4[c, l] + (2.0 / 3.0 * H) * base[c, l]
        start[c, core] = start[c, core] + (2.0 / 3.0 * H) * hout[c]


def cot_two(core_ref, coef, pk2, got, k0s, th, p4, q4, base, vel, l2, ho, hi, k01, k2s, sums):
    core = core_ref[0]
    co = Coef(coef)
    fout, fin = facing(co, vel, core)
    for l in range(2):
        k0 = k0s[l]
        a0 = pk2[2 + l] + got[2 + l]
        theta1 = th[l] + H * (k0 * a0)
        k1 = k0s[2 + l] * jnp.exp(-theta1)
        k01[l] = k0
        k01[2 + l] = k1
        a1 = pk2[l] + got[l]
        theta2 = 0.75 * th[l] + 0.25 * (theta1 + H * (k1 * a1))
        k2 = k0s[2 + l] * jnp.exp(-theta2)
        k2s[l] = k2
        sums[l] = a0
        sums[2 + l] = a1
        for c in range(4):
            p = p4[c, l]
            l2[c, l] = base[c, l] + (2.0 / 3.0 * H) * ((co.rate[c] * k2) * (q4[c, l] - p))
    for c in range(4):
        ho[(c + 2) % 4] = fout[c] * l2[c, core]
        hi[(c + 2) % 4] = fin[c] * l2[c, 1 - core]


def cot_one_base(core_ref, coef, l2, hin, k01, vel, q4, u1, u4, after, l1, part):
    core = core_ref[0]
    co = Coef(coef)
    for c in range(4):
        for l in range(2):
            x = l2[c, l]
            w = (2.0 / 3.0) * q4[c, l] - x
            rest = back(co, l2, vel, core, c, l) + (co.rate[c] * k01[2 + l]) * w
            l1[c, l] = 0.25 * x + (0.25 * H) * rest
        l1[c, 1 - core] = l1[c, 1 - core] + (0.25 * H) * hin[c]
    for l in range(2):
        first = jnp.zeros((N, N), F32)
        zero = jnp.zeros((N, N), F32)
        for c in range(4):
            q = q4[c, l]
            first = first + (co.rate[c] * ((2.0 / 3.0) * q - l2[c, l])) * u1[c, l]
            zero = zero + (co.rate[c] * ((1.0 / 6.0) * q - l1[c, l])) * u4[c, l]
        part[l] = first
        part[2 + l] = zero


def cot_one(core_ref, coef, pk3, got, k01, k2s, sums, l1k, vel, l1, ho, hi, t2s):
    core = core_ref[0]
    co = Coef(coef)
    fout, fin = facing(co, vel, core)
    for l in range(2):
        t2 = (-2.0 / 3.0 * H) * k2s[l] * (pk3[l] + got[l])
        push = (0.25 * H) * (k01[2 + l] * t2)
        t2s[l] = t2
        t2s[2 + l] = sums[l]
        t2s[4 + l] = sums[2 + l]
        t2s[6 + l] = push
        for c in range(4):
            l1[c, l] = l1k[c, l] + (co.rate[c] * co.vol[c]) * push
    for c in range(4):
        ho[(c + 2) % 4] = fout[c] * l1[c, core]
        hi[(c + 2) % 4] = fin[c] * l1[c, 1 - core]


def sums_three(core_ref, coef, base, part, sums, hout, u4, l1, pk4):
    core = core_ref[0]
    co = Coef(coef)
    edge = part[2 + core]
    for c in range(4):
        more = (0.25 * H) * hout[c]
        l1[c, 1 - core] = base[c, 1 - core]
        l1[c, core] = base[c, core] + more
        edge = edge - (co.rate[c] * more) * u4[c, core]
    for l in range(2):
        pk4[l] = part[l]
        pk4[4 + l] = sums[2 + l]
    pk4[3 - core] = part[3 - core]
    pk4[2 + core] = edge


def total_push(core_ref, pk4, got, k01, t2s, tsum, mixed):
    for l in range(2):
        t2 = t2s[l]
        t1 = (-0.25 * H) * k01[2 + l] * ((pk4[l] + got[l]) + t2 * t2s[4 + l])
        both = 0.25 * t2 + t1
        square = pk4[4 + l] + got[4 + l]
        zero = (pk4[2 + l] + got[2 + l]) + both * t2s[2 + l] - t2s[6 + l] * square
        tsum[l] = t2 + t1 - H * (k01[l] * zero)
        mixed[l] = both


def finish_base(core_ref, coef, p4, q4, l2, l1, hin, k01, mixed, vel, out):
    core = core_ref[0]
    co = Coef(coef)
    for l in range(2):
        for c in range(4):
            x = l1[c, l]
            l1s = q4[c, l] * (1.0 / 6.0) + co.vol[c] * mixed[l]
            rest = back(co, l1, vel, core, c, l) + (co.rate[c] * k01[l]) * (l1s - x)
            out[c, l] = (1.0 / 3.0) * p4[c, l] + 0.75 * l2[c, l] + x + H * rest
    for c in range(4):
        out[c, 1 - core] = out[c, 1 - core] + H * hin[c]


def finish(core_ref, base, hout, after, own, msg):
    core = core_ref[0]
    for c in range(4):
        dst = own if c < 2 else msg
        k = 2 * (c % 2)
        dst[k + 1 - core] = base[c, 1 - core]
        dst[k + core] = base[c, core] + H * hout[c]


def write_dep(core_ref, coef, tsum, got, q, dep, buf, sem):
    core = core_ref[0]
    vol = Coef(coef).vol
    copies = []
    for c in range(2):
        for k, (src, half) in enumerate(((tsum, core), (got, 1 - core))):
            for l in range(2):
                buf[c, 2 * half + l] = q[c, 2 * half + l] + vol[c] * src[l]
            there = pl.ds(2 * half, 2)
            copies.append(pltpu.make_async_copy(buf.at[c, there], dep.at[c, there], sem.at[2 * c + k]))
            copies[-1].start()
    for copy in copies:
        copy.wait()


def write_conc(core_ref, own, got, conc, sem):
    core = core_ref[0]
    copies = []
    for c in range(2):
        for k, (src, half) in enumerate(((own, core), (got, 1 - core))):
            copies.append(
                pltpu.make_async_copy(
                    src.at[pl.ds(2 * c, 2)], conc.at[c, pl.ds(2 * half, 2)], sem.at[2 * c + k]
                )
            )
            copies[-1].start()
    for copy in copies:
        copy.wait()


def call(body, outs, scalars, arrays, scratch=(), sems=0, hbm_out=False, size=None):
    smem = pl.BlockSpec(memory_space=pltpu.SMEM)
    vmem = pl.BlockSpec(memory_space=pltpu.VMEM)
    hbm = pl.BlockSpec(memory_space=pltpu.HBM)
    scratch_shapes = [pltpu.VMEM(s, F32) for s in scratch]
    if sems:
        scratch_shapes.append(pltpu.SemaphoreType.DMA((sems,)))
    if size is None:
        size = sum(4 * a.size for a in arrays)
    return pl.pallas_call(
        body,
        out_shape=[jax.ShapeDtypeStruct(s, F32) for s in outs],
        in_specs=[smem] * len(scalars) + [vmem] * len(arrays),
        out_specs=[hbm if hbm_out else vmem] * len(outs),
        scratch_shapes=scratch_shapes,
        compiler_params=pltpu.CompilerParams(vmem_limit_bytes=16 * 1024 * 1024),
        cost_estimate=pl.CostEstimate(
            flops=int(WORK[body.__name__] * 1e9), bytes_accessed=size, transcendentals=0
        ),
        name=body.__name__,
    )(*scalars, *arrays)


def shards(peers, conc, dep, velocity, label, dif, rate, vol, p, q):
    core = (lax.axis_index("size") % 2).astype(jnp.int32)[None]
    swap = [(0, 1), (1, 0), (2, 3), (3, 2)]
    far = [(0, 2), (2, 0), (1, 3), (3, 1)]
    face = []
    for g in range(peers - 1):
        for chip in (0, 2):
            a, b = (chip + 1) * peers + g, chip * peers + g + 1
            face += [(a, b), (b, a)]
    inner = lambda x: lax.ppermute(x, "size", swap)
    across = lambda x: lax.ppermute(x, "size", far)
    outer = lambda x: lax.ppermute(x, ("size", "gz"), face)
    layers = lambda n: (n, N, N)
    eight = (4, 2, N, N)

    msg0, mine, theta, rows = call(
        send_state,
        [layers(9), layers(6), layers(2), (8, N)],
        (core, dif, rate, vol),
        (dep, conc),
        size=0,
    )
    got0 = inner(msg0)
    (msg1,) = call(send_cot, [layers(10)], (core,), (p, q))
    got1 = inner(msg1)
    pk1, ho0, csums, coef, u4, uin = call(
        sums_zero,
        [layers(2), layers(4), layers(4), (16, N), eight, layers(4)],
        (core,),
        (rows, theta, mine, got0),
    )
    gpk1 = across(pk1)
    hu0 = outer(ho0)
    (abase,) = call(step_base, [eight], (core,), (coef, u4, uin, velocity))
    p4, q4, pbase, hop = call(
        cot_base, [eight, eight, eight, layers(4)], (core,), (coef, p, q, got1, velocity)
    )
    hp = outer(hop)
    k0s, th = call(kappa_zero, [layers(4), layers(2)], (core,), (pk1, gpk1, label))
    u1, ho1, hi1, pk2 = call(
        state_one,
        [eight, layers(4), layers(4), layers(4)],
        (core,),
        (coef, abase, hu0, velocity, csums, k0s, u4, pbase),
    )
    gpk2 = across(pk2)
    iu1 = inner(hi1)
    hu1 = outer(ho1)
    part2, wout = call(
        state_two, [layers(4), layers(4)], (core,), (coef, u4, u1, iu1, velocity, p4, q4)
    )
    (l2start,) = call(cot_start, [eight], (core,), (p4, pbase, hp))
    l2, ho2, hi2, k01, k2s, sums = call(
        cot_two,
        [eight, layers(4), layers(4), layers(4), layers(2), layers(4)],
        (core,),
        (coef, pk2, gpk2, k0s, th, p4, q4, l2start, velocity),
    )
    il2 = inner(hi2)
    hl2 = outer(ho2)
    (pk3,) = call(sums_two, [layers(2)], (core,), (part2, wout, hu1, k01))
    gpk3 = across(pk3)
    l1base, part1 = call(
        cot_one_base, [eight, layers(4)], (core,), (coef, l2, il2, k01, velocity, q4, u1, u4, pk3)
    )
    l1k, pk4 = call(
        sums_three, [eight, layers(6)], (core,), (coef, l1base, part1, csums, hl2, u4)
    )
    gpk4 = across(pk4)
    l1, ho3, hi3, t2s = call(
        cot_one,
        [eight, layers(4), layers(4), layers(8)],
        (core,),
        (coef, pk3, gpk3, k01, k2s, sums, l1k, velocity),
    )
    il1 = inner(hi3)
    hl1 = outer(ho3)
    tsum, mixed = call(
        total_push, [layers(2), layers(2)], (core,), (pk4, gpk4, k01, t2s)
    )
    tother = inner(tsum)
    (base,) = call(
        finish_base, [eight], (core,), (coef, p4, q4, l2, l1, il1, k01, mixed, velocity)
    )
    own, msg = call(finish, [layers(4), layers(4)], (core,), (base, hl1, tother))
    theirs = inner(msg)
    state = (2, 4, N, N)
    (dep_out,) = call(
        write_dep, [state], (core,), (coef, tsum, tother, q), [state], 4, hbm_out=True
    )
    (conc_out,) = call(write_conc, [state], (core,), (own, theirs), (), 4, hbm_out=True)
    return conc_out, dep_out


def solution(mesh):
    state = P("size", "gz", None, None)
    flow = P("gz", None, None)
    in_specs = (state, state, flow, flow, P("size"), P("size"), P("size"), state, state)
    body = functools.partial(shards, mesh.shape["gz"])
    return jax.shard_map(
        body, mesh=mesh, in_specs=in_specs, out_specs=(state, state), check_vma=False
    )
```

```python
import functools

import jax
import jax.numpy as jnp
from jax import lax
from jax.experimental import pallas as pl
from jax.experimental.pallas import tpu as pltpu
from jax.sharding import PartitionSpec as P

H = 0.25
SURFACE_EFF = (0.1, 0.6, 1.2, 2.0)
N = 128
WORK = {
    "send_state": 0.01,
    "send_cot": 0.01,
    "sums_zero": 0.01,
    "sums_one": 0.01,
    "step_base": 0.01,
    "cot_base": 0.01,
    "state_one": 0.01,
    "state_two": 0.01,
    "sums_two": 0.01,
    "cot_two": 0.01,
    "cot_one_base": 0.01,
    "cot_one": 0.01,
    "sums_three": 0.01,
    "finish_base": 0.01,
    "finish": 0.01,
    "write_dep": 0.01,
    "write_conc": 0.01,
    "total_push": 0.01,
    "kappa_zero": 2.0,
    "cot_start": 3.0,
}
F32 = jnp.float32


def lateral(x):
    row = lax.broadcasted_iota(jnp.int32, x.shape, 0)
    col = lax.broadcasted_iota(jnp.int32, x.shape, 1)
    up = jnp.where(row > 0, pltpu.roll(x, 1, 0), 0.0)
    down = jnp.where(row < N - 1, pltpu.roll(x, N - 1, 0), 0.0)
    left = jnp.where(col > 0, pltpu.roll(x, 1, 1), 0.0)
    right = jnp.where(col < N - 1, pltpu.roll(x, N - 1, 1), 0.0)
    return (up + down) + (left + right) - 6.0 * x


def efficiency(label):
    out = jnp.zeros(label.shape, F32)
    for k in range(4):
        out = jnp.where(label == k, SURFACE_EFF[k], out)
    return out


class Coef:
    def __init__(self, ref):
        self.dif = [ref[c : c + 1, :] for c in range(4)]
        self.rate = [ref[4 + c : 5 + c, :] for c in range(4)]
        self.vol = [ref[8 + c : 9 + c, :] for c in range(4)]


def send_state(core_ref, dif, rate, vol, dep, conc, msg, mine, theta, rows):
    core = core_ref[0]
    other = 1 - core
    for l in range(2):
        msg[l] = vol[0] * dep[0, 2 * other + l] + vol[1] * dep[1, 2 * other + l]
        theta[l] = vol[0] * dep[0, 2 * core + l] + vol[1] * dep[1, 2 * core + l]
    for c in range(2):
        for l in range(2):
            msg[2 + 3 * c + l] = conc[c, 2 * other + l]
            mine[3 * c + l] = conc[c, 2 * core + l]
        msg[4 + 3 * c] = conc[c, 2 - other]
        mine[3 * c + 2] = conc[c, 2 - core]
    for k, ref in enumerate((dif, rate, vol)):
        for c in range(2):
            row = jnp.full((1, N), ref[c], F32)
            msg[8, 2 * k + c : 2 * k + c + 1, :] = row
            rows[2 * k + c : 2 * k + c + 1, :] = row


def send_cot(core_ref, p, q, msg):
    other = 1 - core_ref[0]
    for c in range(2):
        for l in range(2):
            msg[3 * c + l] = p[c, 2 * other + l]
            msg[6 + 2 * c + l] = q[c, 2 * other + l]
        msg[3 * c + 2] = p[c, 2 - other]


def sums_zero(core_ref, rows, theta, mine, got, pk1, ho, sums, coef, u4, uin):
    core = core_ref[0]
    for k in range(3):
        coef[4 * k : 4 * k + 2, :] = rows[2 * k : 2 * k + 2, :]
        coef[4 * k + 2 : 4 * k + 4, :] = got[8, 2 * k : 2 * k + 2, :]
    co = Coef(coef)
    for l in range(2):
        pk1[l] = got[l] + theta[l]
        total = jnp.zeros((N, N), F32)
        square = jnp.zeros((N, N), F32)
        for c in range(4):
            u = mine[3 * c + l] if c < 2 else got[2 + 3 * (c - 2) + l]
            u4[c, l] = u
            term = (co.vol[c] * co.rate[c]) * u
            total = total + term
            square = square + co.rate[c] * term
        sums[l] = total
        sums[2 + l] = square
    for c in range(4):
        uin[c] = mine[3 * c + 2] if c < 2 else got[4 + 3 * (c - 2)]
        ho[(c + 2) % 4] = u4[c, core]


def advect(co, u4, vel, core, c, l):
    u = u4[c, l]
    out = co.dif[c] * lateral(u) - vel[2 * core + l] * u
    if l == 0:
        return out + co.dif[c] * u4[c, 1]
    return out + (co.dif[c] + vel[2 * core + 1]) * u4[c, 0]


def back(co, x4, vel, core, c, l):
    x = x4[c, l]
    out = co.dif[c] * lateral(x) - vel[2 * core + l] * x
    if l == 0:
        return out + (co.dif[c] + vel[2 * core + 1]) * x4[c, 1]
    return out + co.dif[c] * x4[c, 0]


def facing(co, vel, core):
    low = vel[2 * core]
    out_part = jnp.where(core == 0, low, 0.0)
    in_part = jnp.where(core == 1, low, 0.0)
    return (
        [co.dif[c] + out_part for c in range(4)],
        [co.dif[c] + in_part for c in range(4)],
    )


def step_base(core_ref, coef, u4, uin, vel, after, a4):
    core = core_ref[0]
    co = Coef(coef)
    _, fin = facing(co, vel, core)
    for c in range(4):
        for l in range(2):
            a4[c, l] = u4[c, l] + H * advect(co, u4, vel, core, c, l)
        a4[c, 1 - core] = a4[c, 1 - core] + H * (fin[c] * uin[c])


def cot_base(core_ref, coef, p, q, got, vel, p4, q4, base, ho):
    core = core_ref[0]
    co = Coef(coef)
    fout, _ = facing(co, vel, core)
    above = jnp.where(core == 0, vel[2 - core], 0.0)
    for c in range(4):
        for l in range(2):
            p4[c, l] = p[c, 2 * core + l] if c < 2 else got[3 * (c - 2) + l]
            q4[c, l] = q[c, 2 * core + l] if c < 2 else got[6 + 2 * (c - 2) + l]
        ho[(c + 2) % 4] = fout[c] * p4[c, core]
        for l in range(2):
            base[c, l] = back(co, p4, vel, core, c, l)
        pin = p[c, 2 - core] if c < 2 else got[3 * (c - 2) + 2]
        base[c, 1 - core] = base[c, 1 - core] + (co.dif[c] + above) * pin


def kappa_zero(core_ref, pk1, got, label, k0s, th):
    core = core_ref[0]
    for l in range(2):
        coll = efficiency(label[2 * core + l])
        theta = pk1[l] + got[l]
        k0s[l] = coll * jnp.exp(-theta)
        k0s[2 + l] = coll
        th[l] = theta


def state_one(core_ref, coef, base, hout, vel, sums, k0s, u4, after, u1, ho, hi, pk2):
    core = core_ref[0]
    co = Coef(coef)
    fout, _ = facing(co, vel, core)
    halo = [H * (fout[c] * hout[c]) for c in range(4)]
    extra = jnp.zeros((N, N), F32)
    for c in range(4):
        extra = extra + (co.vol[c] * co.rate[c]) * halo[c]
    for l in range(2):
        total = jnp.zeros((N, N), F32)
        for c in range(4):
            a = base[c, l]
            total = total + (co.vol[c] * co.rate[c]) * a
            u1[c, l] = a - (H * k0s[l]) * (co.rate[c] * u4[c, l])
        pk2[l] = total
        pk2[2 + l] = sums[2 + l]
        pk2[4 + l] = sums[l]
    pk2[core] = pk2[core] + extra
    for c in range(4):
        edge = u1[c, core] + halo[c]
        u1[c, core] = edge
        ho[(c + 2) % 4] = edge
        hi[(c + 2) % 4] = u1[c, 1 - core]


def state_two(core_ref, coef, u4, u1, hin, vel, p4, q4, part, wout):
    core = core_ref[0]
    co = Coef(coef)
    fout, fin = facing(co, vel, core)
    for l in range(2):
        total = jnp.zeros((N, N), F32)
        react = jnp.zeros((N, N), F32)
        for c in range(4):
            u = u1[c, l]
            w = co.rate[c] * (q4[c, l] - p4[c, l])
            total = total + w * (0.75 * u4[c, l] + 0.25 * (u + H * advect(co, u1, vel, core, c, l)))
            react = react + (0.25 * H) * (w * (co.rate[c] * u))
        part[l] = total
        part[2 + l] = react
    edge = part[1 - core]
    for c in range(4):
        scaled = (0.25 * H) * co.rate[c]
        wout[c] = scaled * ((q4[c, core] - p4[c, core]) * fout[c])
        edge = edge + scaled * ((q4[c, 1 - core] - p4[c, 1 - core]) * (fin[c] * hin[c]))
    part[1 - core] = edge


def sums_two(core_ref, part, wout, hout, k01, pk3):
    core = core_ref[0]
    for l in range(2):
        pk3[l] = part[l] - k01[2 + l] * part[2 + l]
    edge = pk3[core]
    for c in range(4):
        edge = edge + wout[c] * hout[c]
    pk3[core] = edge


def cot_start(core_ref, p4, base, hout, start):
    core = core_ref[0]
    for c in range(4):
        for l in range(2):
            start[c, l] = (2.0 / 3.0) * p4[c, l] + (2.0 / 3.0 * H) * base[c, l]
        start[c, core] = start[c, core] + (2.0 / 3.0 * H) * hout[c]


def cot_two(core_ref, coef, pk2, got, k0s, th, p4, q4, base, vel, l2, ho, hi, k01, k2s, sums):
    core = core_ref[0]
    co = Coef(coef)
    fout, fin = facing(co, vel, core)
    for l in range(2):
        k0 = k0s[l]
        a0 = pk2[4 + l] + got[4 + l]
        c0 = pk2[2 + l] + got[2 + l]
        theta1 = th[l] + H * (k0 * a0)
        k1 = k0s[2 + l] * jnp.exp(-theta1)
        k01[l] = k0
        k01[2 + l] = k1
        a1 = (pk2[l] + got[l]) - (H * k0) * c0
        theta2 = 0.75 * th[l] + 0.25 * (theta1 + H * (k1 * a1))
        k2 = k0s[2 + l] * jnp.exp(-theta2)
        k2s[l] = k2
        sums[l] = a0
        sums[2 + l] = a1
        sums[4 + l] = c0
        for c in range(4):
            p = p4[c, l]
            l2[c, l] = base[c, l] + (2.0 / 3.0 * H) * ((co.rate[c] * k2) * (q4[c, l] - p))
    for c in range(4):
        ho[(c + 2) % 4] = fout[c] * l2[c, core]
        hi[(c + 2) % 4] = fin[c] * l2[c, 1 - core]


def cot_one_base(core_ref, coef, l2, hin, k01, vel, q4, u1, u4, l1, part):
    core = core_ref[0]
    co = Coef(coef)
    for c in range(4):
        for l in range(2):
            x = l2[c, l]
            w = (2.0 / 3.0) * q4[c, l] - x
            rest = back(co, l2, vel, core, c, l) + (co.rate[c] * k01[2 + l]) * w
            l1[c, l] = 0.25 * x + (0.25 * H) * rest
        l1[c, 1 - core] = l1[c, 1 - core] + (0.25 * H) * hin[c]
    for l in range(2):
        first = jnp.zeros((N, N), F32)
        zero = jnp.zeros((N, N), F32)
        for c in range(4):
            q = q4[c, l]
            first = first + (co.rate[c] * ((2.0 / 3.0) * q - l2[c, l])) * u1[c, l]
            zero = zero + (co.rate[c] * ((1.0 / 6.0) * q - l1[c, l])) * u4[c, l]
        part[l] = first
        part[2 + l] = zero


def cot_one(core_ref, coef, pk3, got, k01, k2s, sums, l1k, vel, l1, ho, hi, t2s):
    core = core_ref[0]
    co = Coef(coef)
    fout, fin = facing(co, vel, core)
    for l in range(2):
        t2 = (-2.0 / 3.0 * H) * k2s[l] * (pk3[l] + got[l])
        push = (0.25 * H) * (k01[2 + l] * t2)
        t2s[l] = t2
        t2s[2 + l] = sums[l]
        t2s[4 + l] = sums[2 + l]
        t2s[6 + l] = push * sums[4 + l]
        for c in range(4):
            l1[c, l] = l1k[c, l] + (co.rate[c] * co.vol[c]) * push
    for c in range(4):
        ho[(c + 2) % 4] = fout[c] * l1[c, core]
        hi[(c + 2) % 4] = fin[c] * l1[c, 1 - core]


def sums_three(core_ref, coef, base, part, hout, u4, l1, pk4):
    core = core_ref[0]
    co = Coef(coef)
    edge = part[2 + core]
    for c in range(4):
        more = (0.25 * H) * hout[c]
        l1[c, 1 - core] = base[c, 1 - core]
        l1[c, core] = base[c, core] + more
        edge = edge - (co.rate[c] * more) * u4[c, core]
    for l in range(2):
        pk4[l] = part[l]
    pk4[3 - core] = part[3 - core]
    pk4[2 + core] = edge


def total_push(core_ref, pk4, got, k01, t2s, tsum, mixed):
    for l in range(2):
        t2 = t2s[l]
        t1 = (-0.25 * H) * k01[2 + l] * ((pk4[l] + got[l]) + t2 * t2s[4 + l])
        both = 0.25 * t2 + t1
        zero = (pk4[2 + l] + got[2 + l]) + both * t2s[2 + l] - t2s[6 + l]
        tsum[l] = t2 + t1 - H * (k01[l] * zero)
        mixed[l] = both


def finish_base(core_ref, coef, p4, q4, l2, l1, hin, k01, mixed, vel, out, early):
    core = core_ref[0]
    co = Coef(coef)
    for l in range(2):
        for c in range(4):
            x = l1[c, l]
            l1s = q4[c, l] * (1.0 / 6.0) + co.vol[c] * mixed[l]
            rest = back(co, l1, vel, core, c, l) + (co.rate[c] * k01[l]) * (l1s - x)
            out[c, l] = (1.0 / 3.0) * p4[c, l] + 0.75 * l2[c, l] + x + H * rest
    for c in range(4):
        out[c, 1 - core] = out[c, 1 - core] + H * hin[c]
    for c in range(2):
        early[c] = out[2 + c, 1 - core]


def finish(core_ref, base, hout, after, first, own, late):
    core = core_ref[0]
    for c in range(2):
        own[2 * c + 1 - core] = base[c, 1 - core]
        own[2 * c + core] = base[c, core] + H * hout[c]
        late[c] = base[2 + c, core] + H * hout[2 + c]


def write_dep(core_ref, coef, tsum, got, q, dep, buf, sem):
    core = core_ref[0]
    vol = Coef(coef).vol
    copies = []
    for c in range(2):
        for k, (src, half) in enumerate(((tsum, core), (got, 1 - core))):
            for l in range(2):
                buf[c, 2 * half + l] = q[c, 2 * half + l] + vol[c] * src[l]
            there = pl.ds(2 * half, 2)
            copies.append(pltpu.make_async_copy(buf.at[c, there], dep.at[c, there], sem.at[2 * c + k]))
            copies[-1].start()
    for copy in copies:
        copy.wait()


def write_conc(core_ref, own, early, late, conc, sem):
    core = core_ref[0]
    there = 2 * (1 - core)
    copies = []
    for c in range(2):
        pairs = (
            (own.at[pl.ds(2 * c, 2)], conc.at[c, pl.ds(2 * core, 2)]),
            (early.at[c], conc.at[c, there + core]),
            (late.at[c], conc.at[c, there + 1 - core]),
        )
        for k, (src, dst) in enumerate(pairs):
            copies.append(pltpu.make_async_copy(src, dst, sem.at[3 * c + k]))
            copies[-1].start()
    for copy in copies:
        copy.wait()


def call(body, outs, scalars, arrays, scratch=(), sems=0, hbm_out=False, size=None):
    smem = pl.BlockSpec(memory_space=pltpu.SMEM)
    vmem = pl.BlockSpec(memory_space=pltpu.VMEM)
    hbm = pl.BlockSpec(memory_space=pltpu.HBM)
    scratch_shapes = [pltpu.VMEM(s, F32) for s in scratch]
    if sems:
        scratch_shapes.append(pltpu.SemaphoreType.DMA((sems,)))
    if size is None:
        size = sum(4 * a.size for a in arrays)
    return pl.pallas_call(
        body,
        out_shape=[jax.ShapeDtypeStruct(s, F32) for s in outs],
        in_specs=[smem] * len(scalars) + [vmem] * len(arrays),
        out_specs=[hbm if hbm_out else vmem] * len(outs),
        scratch_shapes=scratch_shapes,
        compiler_params=pltpu.CompilerParams(vmem_limit_bytes=16 * 1024 * 1024),
        cost_estimate=pl.CostEstimate(
            flops=int(WORK[body.__name__] * 1e9), bytes_accessed=size, transcendentals=0
        ),
        name=body.__name__,
    )(*scalars, *arrays)


def shards(peers, conc, dep, velocity, label, dif, rate, vol, p, q):
    core = (lax.axis_index("size") % 2).astype(jnp.int32)[None]
    swap = [(0, 1), (1, 0), (2, 3), (3, 2)]
    far = [(0, 2), (2, 0), (1, 3), (3, 1)]
    face = []
    for g in range(peers - 1):
        for chip in (0, 2):
            a, b = (chip + 1) * peers + g, chip * peers + g + 1
            face += [(a, b), (b, a)]
    inner = lambda x: lax.ppermute(x, "size", swap)
    across = lambda x: lax.ppermute(x, "size", far)
    outer = lambda x: lax.ppermute(x, ("size", "gz"), face)
    layers = lambda n: (n, N, N)
    eight = (4, 2, N, N)

    msg0, mine, theta, rows = call(
        send_state,
        [layers(9), layers(6), layers(2), (8, N)],
        (core, dif, rate, vol),
        (dep, conc),
        size=0,
    )
    got0 = inner(msg0)
    (msg1,) = call(send_cot, [layers(10)], (core,), (p, q))
    got1 = inner(msg1)
    pk1, ho0, csums, coef, u4, uin = call(
        sums_zero,
        [layers(2), layers(4), layers(4), (16, N), eight, layers(4)],
        (core,),
        (rows, theta, mine, got0),
    )
    gpk1 = across(pk1)
    hu0 = outer(ho0)
    p4, q4, pbase, hop = call(
        cot_base, [eight, eight, eight, layers(4)], (core,), (coef, p, q, got1, velocity)
    )
    hp = outer(hop)
    (abase,) = call(step_base, [eight], (core,), (coef, u4, uin, velocity, pbase))
    k0s, th = call(kappa_zero, [layers(4), layers(2)], (core,), (pk1, gpk1, label))
    u1, ho1, hi1, pk2 = call(
        state_one,
        [eight, layers(4), layers(4), layers(6)],
        (core,),
        (coef, abase, hu0, velocity, csums, k0s, u4, pbase),
    )
    gpk2 = across(pk2)
    iu1 = inner(hi1)
    hu1 = outer(ho1)
    part2, wout = call(
        state_two, [layers(4), layers(4)], (core,), (coef, u4, u1, iu1, velocity, p4, q4)
    )
    (l2start,) = call(cot_start, [eight], (core,), (p4, pbase, hp))
    l2, ho2, hi2, k01, k2s, sums = call(
        cot_two,
        [eight, layers(4), layers(4), layers(4), layers(2), layers(6)],
        (core,),
        (coef, pk2, gpk2, k0s, th, p4, q4, l2start, velocity),
    )
    il2 = inner(hi2)
    hl2 = outer(ho2)
    (pk3,) = call(sums_two, [layers(2)], (core,), (part2, wout, hu1, k01))
    gpk3 = across(pk3)
    l1base, part1 = call(
        cot_one_base, [eight, layers(4)], (core,), (coef, l2, il2, k01, velocity, q4, u1, u4)
    )
    l1k, pk4 = call(sums_three, [eight, layers(4)], (core,), (coef, l1base, part1, hl2, u4))
    gpk4 = across(pk4)
    l1, ho3, hi3, t2s = call(
        cot_one,
        [eight, layers(4), layers(4), layers(8)],
        (core,),
        (coef, pk3, gpk3, k01, k2s, sums, l1k, velocity),
    )
    il1 = inner(hi3)
    hl1 = outer(ho3)
    tsum, mixed = call(
        total_push, [layers(2), layers(2)], (core,), (pk4, gpk4, k01, t2s)
    )
    tother = inner(tsum)
    base, early = call(
        finish_base, [eight, layers(2)], (core,), (coef, p4, q4, l2, l1, il1, k01, mixed, velocity)
    )
    gearly = inner(early)
    own, late = call(finish, [layers(4), layers(2)], (core,), (base, hl1, tother, gearly))
    glate = inner(late)
    state = (2, 4, N, N)
    (dep_out,) = call(
        write_dep, [state], (core,), (coef, tsum, tother, q), [state], 4, hbm_out=True
    )
    (conc_out,) = call(
        write_conc, [state], (core,), (own, gearly, glate), (), 6, hbm_out=True
    )
    return conc_out, dep_out


def solution(mesh):
    state = P("size", "gz", None, None)
    flow = P("gz", None, None)
    in_specs = (state, state, flow, flow, P("size"), P("size"), P("size"), state, state)
    body = functools.partial(shards, mesh.shape["gz"])
    return jax.shard_map(
        body, mesh=mesh, in_specs=in_specs, out_specs=(state, state), check_vma=False
    )
```
